256 devices in a mesh: tm: 16 (over y, z_hi), gx: 4 (over x), gy: 4 (over z_lo, core).
Axes of the slice: x: 4, y: 4, z: 8 (z_hi: 4, z_lo: 2; z = z_hi * 2 + z_lo), core: 2. Of those that a mesh axis runs over, the one named last changes fastest.
Arguments:
- state: float32 [16, 3, 64, 64, 128], P('tm', None, 'gx', 'gy'), may hold values from -6 to 6
- waveform: float32 [16, 4], P('tm'), may hold values from -9 to 9
- conductivity: float32 [16], replicated, may hold values from 0.1 to 1
- layer_map: int32 [64, 64, 128], P('gx', 'gy'), may hold values from 0 to 15
- loop_mask: int32 [64, 64, 128], P('gx', 'gy'), may hold values 0 or 1
Outputs:
- next_state: float32 [16, 3, 64, 64, 128], P('tm', None, 'gx', 'gy')
The draws below stay inside these ranges and needn't reach their ends.
All inputs are finite; a program needn't handle non-finite values. No bound on the sum of `loop_mask` on one device may be relied on, other than what follows from the above.
Results may differ from the reference program's by a relative error of at most 0.0001.
Values sent between devices are 32-bit elements; how exact they have to be, the bound alone decides.
A program may use at most 128 MiB of HBM per device.

```python
import math
import jax
import jax.numpy as jnp
from jax import lax

NZ = 128
FINE = 4
LAYERS = 16
SLICES = 16
NX = 64
NY = 64


def set_ends(drawn, stream_key, low, top_value):
    spot = [jax.random.randint(jax.random.fold_in(stream_key, axis), (), 0, length) for axis, length in enumerate(drawn.shape)]
    longest = drawn.shape.index(max(drawn.shape))
    neighbour = spot[:longest] + [(spot[longest] + 1) % drawn.shape[longest]] + spot[longest + 1:]
    return drawn.at[tuple(spot)].set(low).at[tuple(neighbour)].set(top_value)


def level_of(own_key, extent, split, low, top_value):
    level = 1.0
    for position, shards_of in split:
        heights = jax.random.uniform(jax.random.fold_in(jax.random.fold_in(own_key, 6), position), (shards_of,), jnp.float32, low / len(split), top_value / len(split))
        level = level * jnp.repeat(jnp.exp(heights), extent[position] // shards_of).reshape((-1,) + (1,) * (len(extent) - 1 - position))
    return level


def noise(key, dims, spread, most, split=(), kind=jnp.bfloat16):
    entries = jax.random.normal(key, dims, jnp.float32) * spread
    if len(split) > 0:
        entries = level_of(key, dims, split, -0.22, 0.18) * entries
    return jnp.clip(entries, min=-most, max=most).astype(kind)


def setup_inputs(seed: int = 0) -> dict:
    seeds = jax.random.split(jax.random.key(seed), 6)
    return {
        "state": noise(seeds[0], (SLICES, 3, NX, NY, NZ), 1.0, 6.0, ((0, 16), (2, 4), (3, 4)), jnp.float32),
        "waveform": noise(seeds[1], (SLICES, FINE), 3.0, 9.0, ((0, 16),), jnp.float32),
        "conductivity": jnp.clip(jnp.exp(jax.random.uniform(seeds[2], (LAYERS,), jnp.float32, math.log(0.1), math.log(1.0))), 0.1, 1.0),
        "layer_map": set_ends(jax.random.randint(seeds[3], (NX, NY, NZ), 0, LAYERS), jax.random.fold_in(seeds[3], 1), 0, LAYERS - 1).astype(jnp.int32),
        "loop_mask": set_ends((jax.random.randint(seeds[4], (NX, NY, NZ), 0, 8) < 1).astype(jnp.int32), jax.random.fold_in(seeds[4], 1), 0, 1),
    }


DT = 0.015


def diff_ahead(values, axis):
    size = values.shape[axis]
    later = lax.slice_in_dim(values, 1, size, axis=axis)
    edge = jnp.zeros_like(lax.slice_in_dim(values, 0, 1, axis=axis))
    return jnp.concatenate([later, edge], axis=axis) - values


def diff_behind(values, axis):
    size = values.shape[axis]
    earlier = lax.slice_in_dim(values, 0, size - 1, axis=axis)
    edge = jnp.zeros_like(lax.slice_in_dim(values, 0, 1, axis=axis))
    return values - jnp.concatenate([edge, earlier], axis=axis)


def curl_local(field):
    field_zero, field_one, field_two = field[0], field[1], field[2]
    twist_zero = diff_ahead(field_two, 1) - diff_ahead(field_one, 2)
    twist_one = diff_ahead(field_zero, 2) - diff_ahead(field_two, 0)
    twist_two = diff_ahead(field_one, 0) - diff_ahead(field_zero, 1)
    back_zero = diff_behind(twist_two, 1) - diff_behind(twist_one, 2)
    back_one = diff_behind(twist_zero, 2) - diff_behind(twist_two, 0)
    back_two = diff_behind(twist_one, 0) - diff_behind(twist_zero, 1)
    return jnp.stack([back_zero, back_one, back_two])


def curl_curl(field):
    padded = jnp.pad(field, ((0, 0), (1, 1), (1, 1), (0, 0)))
    return curl_local(padded)[:, 1:-1, 1:-1]


def fine_step(field, kappa, drive, pulse):
    moved = field - (DT * kappa) * curl_curl(field)
    return jnp.stack([moved[0] - (DT * pulse) * drive, moved[1], moved[2]])


def coarse_step(coarse, coarse_kappa):
    return coarse - (4.0 * DT * coarse_kappa) * (curl_curl(coarse) * 0.25)


def restrict(field):
    comps, size_a, size_b, size_c = field.shape
    blocks = field.reshape(comps, size_a // 2, 2, size_b // 2, 2, size_c // 2, 2)
    return jnp.mean(blocks, axis=(2, 4, 6))


def prolong(coarse):
    return jnp.repeat(jnp.repeat(jnp.repeat(coarse, 2, axis=1), 2, axis=2), 2, axis=3)


def reference(state, waveform, conductivity, layer_map, loop_mask):
    kappa = jnp.take(1.0 / conductivity, layer_map, axis=0)
    drive = kappa * loop_mask.astype(jnp.float32)
    coarse_kappa = restrict(kappa[None])[0]

    def advance(coarse, inputs):
        slice_state, pulses = inputs
        field = slice_state
        for turn in range(FINE):
            field = fine_step(field, kappa, drive, pulses[turn])
        start = restrict(slice_state)
        result = field + prolong(coarse_step(coarse - start, coarse_kappa))
        following = coarse_step(coarse, coarse_kappa) + (restrict(field) - coarse_step(start, coarse_kappa))
        return following, result

    final_coarse, outputs = lax.scan(advance, restrict(state[0]), (state, waveform))
    return outputs
```

```python
import jax
import jax.numpy as jnp
from jax import lax
from jax.experimental import pallas as pl
from jax.experimental.pallas import tpu as pltpu
from jax.sharding import PartitionSpec as P

DT = 0.015
MESH = pl.DeviceIdType.MESH
HIGHEST = lax.Precision.HIGHEST
DIRS = [(di, dj) for di in (-1, 0, 1) for dj in (-1, 0, 1) if (di, dj) != (0, 0)]
F32 = jnp.float32


def shifts(rows, last):
    lane = lax.broadcasted_iota(jnp.int32, (rows, 128), 1)
    keep_up = lane < last
    keep_down = lane > 0

    def col_next(x):
        return pltpu.roll(x, rows - 1, 0)

    def col_prev(x):
        return pltpu.roll(x, 1, 0)

    def z_next(x):
        return jnp.where(keep_up, pltpu.roll(x, 127, 1), 0.0)

    def z_prev(x):
        return jnp.where(keep_down, pltpu.roll(x, 1, 1), 0.0)

    return col_next, col_prev, z_next, z_prev


def sweep(src, dst, low, high, last, finish):
    col_next, col_prev, z_next, z_prev = shifts(24, last)

    def twists(i):
        v0, v1, v2 = src[0, i], src[1, i], src[2, i]
        h1 = (z_next(v0) - v0) - (src[2, i + 1] - v2)
        h2 = (src[1, i + 1] - v1) - (col_next(v0) - v0)
        return v0, v1, v2, h1, h2

    def row(i, carry):
        h1_before, h2_before = carry
        v0, v1, v2, h1, h2 = twists(i)
        h0 = (col_next(v2) - v2) - (z_next(v1) - v1)
        k0 = (h2 - col_prev(h2)) - (h1 - z_prev(h1))
        k1 = (h0 - z_prev(h0)) - (h2 - h2_before)
        k2 = (h1 - h1_before) - (h0 - col_prev(h0))
        finish(dst, i, (v0, v1, v2), (k0, k1, k2))
        return h1, h2

    before = twists(low - 1)
    lax.fori_loop(low, high, row, (before[3], before[4]))


def restrict(read, comps, sums):
    for half in range(2):
        for c in range(comps):
            for k in range(4):
                i = 2 * (4 * half + k)
                sums[half, c, k] = (read(c, i, 0) + read(c, i, 1)) + (read(c, i + 1, 0) + read(c, i + 1, 1))
    z = lax.broadcasted_iota(jnp.int32, (128, 128), 0)
    lane = lax.broadcasted_iota(jnp.int32, (128, 128), 1)
    total = 0.0
    for half in range(2):
        pick = jnp.where(lane == z // 2 + 64 * half, 0.125, 0.0).astype(F32)
        x = sums[half, 0:comps].reshape(comps * 32, 128)
        total = total + jnp.dot(x, pick, precision=HIGHEST, preferred_element_type=F32)
    return total.reshape(comps, 4, 8, 128)


def kernel(
    state, wave, cond, layer, mask, out,
    w, v, near, far, lay, msk, sums, ck, exa, exb, rs, rs_next, ps, arrived, c0, c1, ckf, acc,
    in_sem, fine_send, fine_recv, ck_send, ck_recv, a_send, a_recv, b_send, b_recv, rs_send, rs_recv, p_send, p_recv,
):
    n, gx, gy = lax.axis_index("tm"), lax.axis_index("gx"), lax.axis_index("gy")
    slices = 16

    def beside(di, dj):
        return (n, lax.rem(gx + di + 4, 4), lax.rem(gy + dj + 4, 4))

    def remote(src, dst, ssem, rsem, device):
        return pltpu.make_async_remote_copy(
            src_ref=src, dst_ref=dst, send_sem=ssem, recv_sem=rsem, device_id=device, device_id_type=MESH
        )

    loads = [
        pltpu.make_async_copy(state.at[0], w.at[0:3, 4:20, 0:16], in_sem.at[0]),
        pltpu.make_async_copy(layer, lay, in_sem.at[1]),
        pltpu.make_async_copy(mask, msk, in_sem.at[2]),
    ]
    for load in loads:
        load.start()

    barrier = pltpu.get_barrier_semaphore()
    for di, dj in DIRS:
        pl.semaphore_signal(barrier, inc=1, device_id=beside(di, dj), device_id_type=MESH)
    for m in range(1, slices):
        pl.semaphore_signal(barrier, inc=1, device_id=(lax.rem(n + m, slices), gx, gy), device_id_type=MESH)

    for load in loads:
        load.wait()

    for i in range(16):
        chosen = jnp.full((16, 128), cond[0], F32)
        for level in range(1, 16):
            chosen = jnp.where(lay[i] == level, cond[level], chosen)
        scaled = DT / chosen
        w[3, 4 + i, 0:16] = scaled
        w[4, 4 + i, 0:16] = scaled * msk[i].astype(F32)
    near[0] = w[:, 4:20, 0:4]
    near[1] = w[:, 4:20, 12:16]

    pl.semaphore_wait(barrier, len(DIRS) + slices - 1)

    def fine_ends(di, dj):
        if dj == 0:
            return (w.at[:, 4:8, 0:16], w.at[:, 20:24, 0:16]) if di < 0 else (w.at[:, 16:20, 0:16], w.at[:, 0:4, 0:16])
        side = 0 if dj < 0 else 1
        if di == 0:
            return near.at[side], far.at[side, :, 4:20]
        if di < 0:
            return near.at[side, :, 0:4], far.at[side, :, 20:24]
        return near.at[side, :, 12:16], far.at[side, :, 0:4]

    fine_copies = []
    for k, (di, dj) in enumerate(DIRS):
        source, target = fine_ends(di, dj)
        copy = remote(source, target, fine_send.at[k], fine_recv.at[k], beside(di, dj))
        copy.start()
        fine_copies.append(copy)

    def exchange(buf, ssem, rsem):
        copies = []
        for k, (di, dj) in enumerate(DIRS):
            copy = remote(buf.at[1, 1], buf.at[1 - di, 1 - dj], ssem.at[k], rsem.at[k], beside(di, dj))
            copy.start()
            copies.append(copy)
        return copies

    ck[1, 1] = restrict(lambda c, i, b: w[3, 4 + i, pl.ds(b, 8, stride=2)], 1, sums)[0]
    ck_copies = exchange(ck, ck_send, ck_recv)
    rs[...] = restrict(lambda c, i, b: w[c, 4 + i, pl.ds(b, 8, stride=2)], 3, sums)
    rs_copy = remote(rs, rs_next, rs_send.at[0], rs_recv.at[0], (lax.rem(n + slices - 1, slices), gx, gy))
    rs_copy.start()

    for copy in fine_copies:
        copy.wait()

    inside = {
        (-1, 0): jnp.where(gx > 0, 1.0, 0.0).astype(F32),
        (1, 0): jnp.where(gx < 3, 1.0, 0.0).astype(F32),
        (0, -1): jnp.where(gy > 0, 1.0, 0.0).astype(F32),
        (0, 1): jnp.where(gy < 3, 1.0, 0.0).astype(F32),
    }
    for c in range(5):
        w[c, :, 16:20] = far[0, c] * inside[0, 1]
        w[c, :, 20:24] = far[1, c] * inside[0, -1]

    @pl.when(gx == 0)
    def _():
        w[:, 0:4] = jnp.zeros((5, 4, 24, 128), F32)

    @pl.when(gx == 3)
    def _():
        w[:, 20:24] = jnp.zeros((5, 4, 24, 128), F32)

    for step in range(4):
        pulse = wave[0, step]

        def finish(dst, i, values, curls, pulse=pulse):
            scaled = w[3, i]
            dst[0, i] = values[0] - scaled * curls[0] - pulse * w[4, i]
            dst[1, i] = values[1] - scaled * curls[1]
            dst[2, i] = values[2] - scaled * curls[2]

        src, dst = (w, v) if step % 2 == 0 else (v, w)
        sweep(src, dst, 1 + step, 23 - step, 127, finish)

    end = restrict(lambda c, i, b: w[c, 4 + i, pl.ds(b, 8, stride=2)], 3, sums)
    rs_copy.wait()
    exa[1, 1] = end - rs_next[...]
    a_copies = exchange(exa, a_send, a_recv)

    def flag(ei, ej):
        value = 1.0
        if ei != 0:
            value = value * inside[ei, 0]
        if ej != 0:
            value = value * inside[0, ej]
        return value

    tiles = {0: 0, 1: 1, -1: 2}

    def spread(block, scale, put, ei, ej):
        block = block * scale
        put(8 + 8 * ei, tiles[ej], block)
        put(12 + 8 * ei, tiles[ej], pltpu.roll(block, 64, block.ndim - 1))

    for copy in ck_copies:
        copy.wait()
    for ei in (-1, 0, 1):
        for ej in (-1, 0, 1):

            def put_kappa(row, tile, block):
                ckf[row : row + 4, 8 * tile : 8 * tile + 8] = block

            spread(ck[ei + 1, ej + 1], flag(ei, ej), put_kappa, ei, ej)

    def unpack(buf):
        for ei in (-1, 0, 1):
            for ej in (-1, 0, 1):
                for c in range(3):

                    def put(row, tile, block, c=c):
                        c0[c, row : row + 4, 8 * tile : 8 * tile + 8] = block

                    spread(buf[ei + 1, ej + 1, c], flag(ei, ej), put, ei, ej)

    left_half = lax.broadcasted_iota(jnp.int32, (4, 8, 128), 2) < 64

    def finish_coarse(dst, i, values, curls):
        scaled = ckf[i]
        for c in range(3):
            dst[c, i] = values[c] - scaled * curls[c]

    def power(m):
        return remote(
            ps.at[m - 1], arrived.at[m - 1], p_send.at[m - 1], p_recv.at[m - 1], (lax.rem(n + m, slices), gx, gy)
        )

    def one(src, dst, local, m):
        sweep(src, dst, local, 24 - local, 63, finish_coarse)
        for c in range(3):
            ps[m - 1, c] = jnp.where(left_half, dst[c, 8:12, 0:8], pltpu.roll(dst[c, 12:16, 0:8], 64, 2))

        @pl.when(n + m < slices)
        def _():
            power(m).start()

    def phase(first):
        def two(t, carry):
            one(c0, c1, 2 * t + 1, first + 2 * t + 1)
            one(c1, c0, 2 * t + 2, first + 2 * t + 2)
            return carry

        lax.fori_loop(0, 4, two, 0)

    for copy in a_copies:
        copy.wait()
    unpack(exa)
    phase(0)
    exb[1, 1] = ps[7]
    b_copies = exchange(exb, b_send, b_recv)
    for copy in b_copies:
        copy.wait()
    unpack(exb)
    phase(8)

    acc[...] = jnp.zeros_like(acc)

    def gather(m, carry):
        @pl.when(m <= n)
        def _():
            power(m).wait_recv()
            acc[...] += arrived[m - 1]

        @pl.when(n + m < slices)
        def _():
            power(m).wait_send()

        return carry

    lax.fori_loop(1, slices, gather, 0)

    z = lax.broadcasted_iota(jnp.int32, (128, 128), 1)
    lane = lax.broadcasted_iota(jnp.int32, (128, 128), 0)
    packed = acc[...].reshape(96, 128)
    for half in range(2):
        pick = jnp.where(lane == z // 2 + 64 * half, 1.0, 0.0).astype(F32)
        wide = jnp.dot(packed, pick, precision=HIGHEST, preferred_element_type=F32).reshape(3, 4, 8, 128)
        for c in range(3):
            for k in range(4):
                for a in range(2):
                    i = 2 * (4 * half + k) + a
                    for b in range(2):
                        cells = pl.ds(b, 8, stride=2)
                        out[0, c, i, cells] = w[c, 4 + i, cells] + wide[c, k]


def body(state, waveform, conductivity, layer_map, loop_mask):
    any_space = pl.BlockSpec(memory_space=pl.ANY)
    smem = pl.BlockSpec(memory_space=pltpu.SMEM)
    vmem = lambda *shape: pltpu.VMEM(shape, F32)
    dma = lambda count: pltpu.SemaphoreType.DMA((count,))
    return pl.pallas_call(
        kernel,
        out_shape=jax.ShapeDtypeStruct(state.shape, F32),
        in_specs=[any_space, smem, smem, any_space, any_space],
        out_specs=pl.BlockSpec(memory_space=pltpu.VMEM),
        scratch_shapes=[
            vmem(5, 24, 24, 128),
            vmem(3, 24, 24, 128),
            vmem(2, 5, 16, 4, 128),
            vmem(2, 5, 24, 4, 128),
            pltpu.VMEM((16, 16, 128), jnp.int32),
            pltpu.VMEM((16, 16, 128), jnp.int32),
            vmem(2, 3, 4, 8, 128),
            vmem(3, 3, 4, 8, 128),
            vmem(3, 3, 3, 4, 8, 128),
            vmem(3, 3, 3, 4, 8, 128),
            vmem(3, 4, 8, 128),
            vmem(3, 4, 8, 128),
            vmem(16, 3, 4, 8, 128),
            vmem(16, 3, 4, 8, 128),
            vmem(3, 24, 24, 128),
            vmem(3, 24, 24, 128),
            vmem(24, 24, 128),
            vmem(3, 4, 8, 128),
            dma(3),
            dma(8), dma(8), dma(8), dma(8), dma(8), dma(8), dma(8), dma(8),
            dma(1), dma(1), dma(16), dma(16),
        ],
        compiler_params=pltpu.CompilerParams(
            collective_id=0, has_side_effects=True, vmem_limit_bytes=40 * 1024 * 1024
        ),
        name="parareal",
    )(state, waveform, conductivity, layer_map, loop_mask)


def solution(mesh):
    placed = (
        P("tm", None, "gx", "gy", None),
        P("tm", None),
        P(),
        P("gx", "gy", None),
        P("gx", "gy", None),
    )
    return jax.shard_map(
        body, mesh=mesh, in_specs=placed, out_specs=P("tm", None, "gx", "gy", None), check_vma=False
    )
```

```python
import jax
import jax.numpy as jnp
from jax import lax
from jax.experimental import pallas as pl
from jax.experimental.pallas import tpu as pltpu
from jax.sharding import PartitionSpec as P

DT = 0.015
GROUP = 8
MESH = pl.DeviceIdType.MESH
HIGHEST = lax.Precision.HIGHEST
DIRS = [(di, dj) for di in (-1, 0, 1) for dj in (-1, 0, 1) if (di, dj) != (0, 0)]
F32 = jnp.float32


def shifts(rows, last):
    lane = lax.broadcasted_iota(jnp.int32, (rows, 128), 1)
    keep_up = lane < last
    keep_down = lane > 0

    def col_next(x):
        return pltpu.roll(x, rows - 1, 0)

    def col_prev(x):
        return pltpu.roll(x, 1, 0)

    def z_next(x):
        return jnp.where(keep_up, pltpu.roll(x, 127, 1), 0.0)

    def z_prev(x):
        return jnp.where(keep_down, pltpu.roll(x, 1, 1), 0.0)

    return col_next, col_prev, z_next, z_prev


def sweep(src, dst, low, high, last, finish):
    col_next, col_prev, z_next, z_prev = shifts(24, last)

    def twists(i):
        v0, v1, v2 = src[0, i], src[1, i], src[2, i]
        h1 = (z_next(v0) - v0) - (src[2, i + 1] - v2)
        h2 = (src[1, i + 1] - v1) - (col_next(v0) - v0)
        return v0, v1, v2, h1, h2

    def row(i, carry):
        h1_before, h2_before = carry
        v0, v1, v2, h1, h2 = twists(i)
        h0 = (col_next(v2) - v2) - (z_next(v1) - v1)
        k0 = (h2 - col_prev(h2)) - (h1 - z_prev(h1))
        k1 = (h0 - z_prev(h0)) - (h2 - h2_before)
        k2 = (h1 - h1_before) - (h0 - col_prev(h0))
        finish(dst, i, (v0, v1, v2), (k0, k1, k2))
        return h1, h2

    before = twists(low - 1)
    carry = (before[3], before[4])

    def rows(t, carry):
        for k in range(GROUP):
            carry = row(low + GROUP * t + k, carry)
        return carry

    groups, rest = divmod(high - low, GROUP)
    carry = lax.fori_loop(0, groups, rows, carry)
    for k in range(rest):
        carry = row(low + GROUP * groups + k, carry)


def restrict(read, comps, sums):
    for half in range(2):
        for c in range(comps):
            for k in range(4):
                i = 2 * (4 * half + k)
                sums[half, c, k] = (read(c, i, 0) + read(c, i, 1)) + (read(c, i + 1, 0) + read(c, i + 1, 1))
    z = lax.broadcasted_iota(jnp.int32, (128, 128), 0)
    lane = lax.broadcasted_iota(jnp.int32, (128, 128), 1)
    total = 0.0
    for half in range(2):
        pick = jnp.where(lane == z // 2 + 64 * half, 0.125, 0.0).astype(F32)
        x = sums[half, 0:comps].reshape(comps * 32, 128)
        total = total + jnp.dot(x, pick, precision=HIGHEST, preferred_element_type=F32)
    return total.reshape(comps, 4, 8, 128)


def kernel(
    state, wave, cond, layer, mask, out,
    w, v, near, far, lay, msk, sums, ck, exa, exb, rs, rs_next, ps, arrived, zs, zarr, c0, c1, ckf, acc,
    in_sem, fine_send, fine_recv, ck_send, ck_recv, a_send, a_recv, b_send, b_recv, rs_send, rs_recv, p_send, p_recv,
    z_send, z_recv, linked,
):
    n, gx, gy = lax.axis_index("tm"), lax.axis_index("gx"), lax.axis_index("gy")
    slices = 16

    plane, column = n // 4, lax.rem(n, 4)

    def beside(di, dj):
        return (n, gx + di, gy + dj)

    def exists(di, dj):
        return (gx + di >= 0) & (gx + di < 4) & (gy + dj >= 0) & (gy + dj < 4)

    def along(planes, columns):
        return (4 * lax.rem(plane + planes + 4, 4) + lax.rem(column + columns + 4, 4), gx, gy)

    def remote(src, dst, ssem, rsem, device):
        return pltpu.make_async_remote_copy(
            src_ref=src, dst_ref=dst, send_sem=ssem, recv_sem=rsem, device_id=device, device_id_type=MESH
        )

    loads = [
        pltpu.make_async_copy(state.at[0], w.at[0:3, 4:20, 0:16], in_sem.at[0]),
        pltpu.make_async_copy(layer, lay, in_sem.at[1]),
        pltpu.make_async_copy(mask, msk, in_sem.at[2]),
    ]
    for load in loads:
        load.start()

    barrier = pltpu.get_barrier_semaphore()
    for di, dj in DIRS:

        @pl.when(exists(di, dj))
        def _(di=di, dj=dj):
            pl.semaphore_signal(barrier, inc=1, device_id=beside(di, dj), device_id_type=MESH)

    for planes, columns in ((1, 0), (2, 0), (3, 0), (0, 1), (0, 3)):
        pl.semaphore_signal(barrier, inc=1, device_id=along(planes, columns), device_id_type=MESH)

    @pl.when(gx == 0)
    def _():
        for buf in (ck, exa, exb):
            buf[0] = jnp.zeros(buf.shape[1:], F32)

    @pl.when(gx == 3)
    def _():
        for buf in (ck, exa, exb):
            buf[2] = jnp.zeros(buf.shape[1:], F32)

    @pl.when(gy == 0)
    def _():
        for buf in (ck, exa, exb):
            buf[:, 0] = jnp.zeros((3,) + buf.shape[2:], F32)
        far[1] = jnp.zeros(far.shape[1:], F32)

    @pl.when(gy == 3)
    def _():
        for buf in (ck, exa, exb):
            buf[:, 2] = jnp.zeros((3,) + buf.shape[2:], F32)
        far[0] = jnp.zeros(far.shape[1:], F32)

    for load in loads:
        load.wait()

    for i in range(16):
        chosen = jnp.full((16, 128), cond[0], F32)
        for level in range(1, 16):
            chosen = jnp.where(lay[i] == level, cond[level], chosen)
        scaled = DT / chosen
        w[3, 4 + i, 0:16] = scaled
        w[4, 4 + i, 0:16] = scaled * msk[i].astype(F32)
    near[0] = w[:, 4:20, 0:4]
    near[1] = w[:, 4:20, 12:16]

    two, three = jnp.int32(2), jnp.int32(3)
    in_x = jnp.where((gx == 0) | (gx == 3), two, three)
    in_y = jnp.where((gy == 0) | (gy == 3), two, three)
    pl.semaphore_wait(barrier, in_x * in_y - 1 + 5)
    pl.semaphore_signal(linked, inc=1, device_id=along(0, 1), device_id_type=MESH)

    def fine_ends(di, dj):
        if dj == 0:
            return (w.at[:, 4:8, 0:16], w.at[:, 20:24, 0:16]) if di < 0 else (w.at[:, 16:20, 0:16], w.at[:, 0:4, 0:16])
        side = 0 if dj < 0 else 1
        if di == 0:
            return near.at[side], far.at[side, :, 4:20]
        if di < 0:
            return near.at[side, :, 0:4], far.at[side, :, 20:24]
        return near.at[side, :, 12:16], far.at[side, :, 0:4]

    def swap(ends, ssem, rsem):
        copies = []
        for k, (di, dj) in enumerate(DIRS):
            source, target = ends(di, dj)
            copy = remote(source, target, ssem.at[k], rsem.at[k], beside(di, dj))
            pl.when(exists(di, dj))(copy.start)
            copies.append((copy, di, dj))

        def finish():
            for copy, di, dj in copies:
                pl.when(exists(-di, -dj))(copy.wait_recv)
            for copy, di, dj in copies:
                pl.when(exists(di, dj))(copy.wait_send)

        return finish

    def exchange(buf, ssem, rsem):
        return swap(lambda di, dj: (buf.at[1, 1], buf.at[1 - di, 1 - dj]), ssem, rsem)

    fine_arrive = swap(fine_ends, fine_send, fine_recv)
    ck[1, 1] = restrict(lambda c, i, b: w[3, 4 + i, pl.ds(b, 8, stride=2)], 1, sums)[0]
    ck_arrive = exchange(ck, ck_send, ck_recv)
    rs[...] = restrict(lambda c, i, b: w[c, 4 + i, pl.ds(b, 8, stride=2)], 3, sums)
    rs_copy = remote(rs, rs_next, rs_send.at[0], rs_recv.at[0], (lax.rem(n + slices - 1, slices), gx, gy))
    pl.semaphore_wait(linked, 1)
    pl.when(n > 0)(rs_copy.start)

    fine_arrive()
    for c in range(5):
        w[c, :, 16:20] = far[0, c]
        w[c, :, 20:24] = far[1, c]

    @pl.when(gx == 0)
    def _():
        w[:, 0:4] = jnp.zeros((5, 4, 24, 128), F32)

    @pl.when(gx == 3)
    def _():
        w[:, 20:24] = jnp.zeros((5, 4, 24, 128), F32)

    for step in range(4):
        pulse = wave[0, step]

        def finish(dst, i, values, curls, pulse=pulse):
            scaled = w[3, i]
            dst[0, i] = values[0] - scaled * curls[0] - pulse * w[4, i]
            dst[1, i] = values[1] - scaled * curls[1]
            dst[2, i] = values[2] - scaled * curls[2]

        src, dst = (w, v) if step % 2 == 0 else (v, w)
        sweep(src, dst, 1 + step, 23 - step, 127, finish)

    end = restrict(lambda c, i, b: w[c, 4 + i, pl.ds(b, 8, stride=2)], 3, sums)
    pl.when(n < slices - 1)(rs_copy.wait_recv)
    pl.when(n > 0)(rs_copy.wait_send)
    exa[1, 1] = end - rs_next[...]
    a_arrive = exchange(exa, a_send, a_recv)

    tiles = {0: 0, 1: 1, -1: 2}

    def spread(block, put, ei, ej):
        put(8 + 8 * ei, tiles[ej], block)
        put(12 + 8 * ei, tiles[ej], pltpu.roll(block, 64, block.ndim - 1))

    ck_arrive()
    for ei in (-1, 0, 1):
        for ej in (-1, 0, 1):

            def put_kappa(row, tile, block):
                ckf[row : row + 4, 8 * tile : 8 * tile + 8] = block

            spread(ck[ei + 1, ej + 1], put_kappa, ei, ej)

    def unpack(buf):
        for ei in (-1, 0, 1):
            for ej in (-1, 0, 1):
                for c in range(3):

                    def put(row, tile, block, c=c):
                        c0[c, row : row + 4, 8 * tile : 8 * tile + 8] = block

                    spread(buf[ei + 1, ej + 1, c], put, ei, ej)

    left_half = lax.broadcasted_iota(jnp.int32, (4, 8, 128), 2) < 64

    def finish_coarse(dst, i, values, curls):
        scaled = ckf[i]
        for c in range(3):
            dst[c, i] = values[c] - scaled * curls[c]

    def carried(b):
        return jnp.where(column + b >= 4, jnp.int32(1), jnp.int32(0))

    def power(m):
        planes = m // 4 + carried(m % 4)
        copy = remote(ps.at[m - 1], arrived.at[m - 1], p_send.at[m - 1], p_recv.at[m - 1], along(planes, 0))
        sent = (planes > 0) & (plane + planes < 4)
        received = (planes > 0) & (plane - planes >= 0)
        return copy, sent, received

    def one(src, dst, local, m):
        sweep(src, dst, local, 24 - local, 63, finish_coarse)
        for c in range(3):
            ps[m - 1, c] = jnp.where(left_half, dst[c, 8:12, 0:8], pltpu.roll(dst[c, 12:16, 0:8], 64, 2))

        copy, sent, _ = power(m)
        pl.when(sent)(copy.start)

    def phase(first):
        for step in range(1, 9):
            if first + step < slices:
                src, dst = (c0, c1) if step % 2 else (c1, c0)
                one(src, dst, step, first + step)

    a_arrive()
    unpack(exa)
    phase(0)

    @pl.when(n < slices - 9)
    def _():
        exb[1, 1] = ps[7]
        exchange(exb, b_send, b_recv)()
        unpack(exb)
        phase(8)

    def across(b):
        return remote(zs.at[b - 1], zarr.at[b - 1], z_send.at[b - 1], z_recv.at[b - 1], along(0, b))

    for b in (1, 2, 3):
        kept = plane >= carried(b)

        @pl.when(carried(b) == 0)
        def _(b=b):
            zs[b - 1] = ps[b - 1]

        @pl.when(carried(b) == 1)
        def _(b=b):
            zs[b - 1] = jnp.zeros(zs.shape[1:], F32)

        for m in range(b, slices, 4):
            copy, _, received = power(m)

            @pl.when(received)
            def _(copy=copy, m=m, b=b):
                copy.wait_recv()
                zs[b - 1] += arrived[m - 1]

        pl.when(kept)(across(b).start)

    acc[...] = jnp.zeros_like(acc)
    for m in (4, 8, 12):
        copy, _, received = power(m)

        @pl.when(received)
        def _(copy=copy, m=m):
            copy.wait_recv()
            acc[...] += arrived[m - 1]

    for b in (1, 2, 3):
        @pl.when((column >= b) | (plane > 0))
        def _(b=b):
            across(b).wait_recv()
            acc[...] += zarr[b - 1]

    for m in range(1, slices):
        copy, sent, _ = power(m)
        pl.when(sent)(copy.wait_send)
    for b in (1, 2, 3):
        pl.when(plane >= carried(b))(across(b).wait_send)

    z = lax.broadcasted_iota(jnp.int32, (128, 128), 1)
    lane = lax.broadcasted_iota(jnp.int32, (128, 128), 0)
    packed = acc[...].reshape(96, 128)
    for half in range(2):
        pick = jnp.where(lane == z // 2 + 64 * half, 1.0, 0.0).astype(F32)
        wide = jnp.dot(packed, pick, precision=HIGHEST, preferred_element_type=F32).reshape(3, 4, 8, 128)
        for c in range(3):
            for k in range(4):
                for a in range(2):
                    i = 2 * (4 * half + k) + a
                    for b in range(2):
                        cells = pl.ds(b, 8, stride=2)
                        out[0, c, i, cells] = w[c, 4 + i, cells] + wide[c, k]


def body(state, waveform, conductivity, layer_map, loop_mask):
    any_space = pl.BlockSpec(memory_space=pl.ANY)
    smem = pl.BlockSpec(memory_space=pltpu.SMEM)
    vmem = lambda *shape: pltpu.VMEM(shape, F32)
    dma = lambda count: pltpu.SemaphoreType.DMA((count,))
    return pl.pallas_call(
        kernel,
        out_shape=jax.ShapeDtypeStruct(state.shape, F32),
        in_specs=[any_space, smem, smem, any_space, any_space],
        out_specs=pl.BlockSpec(memory_space=pltpu.VMEM),
        scratch_shapes=[
            vmem(5, 24, 24, 128),
            vmem(3, 24, 24, 128),
            vmem(2, 5, 16, 4, 128),
            vmem(2, 5, 24, 4, 128),
            pltpu.VMEM((16, 16, 128), jnp.int32),
            pltpu.VMEM((16, 16, 128), jnp.int32),
            vmem(2, 3, 4, 8, 128),
            vmem(3, 3, 4, 8, 128),
            vmem(3, 3, 3, 4, 8, 128),
            vmem(3, 3, 3, 4, 8, 128),
            vmem(3, 4, 8, 128),
            vmem(3, 4, 8, 128),
            vmem(16, 3, 4, 8, 128),
            vmem(16, 3, 4, 8, 128),
            vmem(3, 3, 4, 8, 128),
            vmem(3, 3, 4, 8, 128),
            vmem(3, 24, 24, 128),
            vmem(3, 24, 24, 128),
            vmem(24, 24, 128),
            vmem(3, 4, 8, 128),
            dma(3),
            dma(8), dma(8), dma(8), dma(8), dma(8), dma(8), dma(8), dma(8),
            dma(1), dma(1), dma(16), dma(16), dma(3), dma(3), pltpu.SemaphoreType.REGULAR,
        ],
        compiler_params=pltpu.CompilerParams(
            collective_id=0, has_side_effects=True, vmem_limit_bytes=60 * 1024 * 1024
        ),
        name="parareal",
    )(state, waveform, conductivity, layer_map, loop_mask)


def solution(mesh):
    placed = (
        P("tm", None, "gx", "gy", None),
        P("tm", None),
        P(),
        P("gx", "gy", None),
        P("gx", "gy", None),
    )
    return jax.shard_map(
        body, mesh=mesh, in_specs=placed, out_specs=P("tm", None, "gx", "gy", None), check_vma=False
    )
```

```python
import jax
import jax.numpy as jnp
from jax import lax
from jax.experimental import pallas as pl
from jax.experimental.pallas import tpu as pltpu
from jax.sharding import PartitionSpec as P

DT = 0.015
GROUP = 8
MESH = pl.DeviceIdType.MESH
HIGHEST = lax.Precision.HIGHEST
DIRS = [(-1, 0), (1, 0), (-1, -1), (1, 1), (-1, 1), (1, -1), (0, -1), (0, 1)]
F32 = jnp.float32


def shifts(rows, depth):
    cell = lax.rem(lax.broadcasted_iota(jnp.int32, (rows, 128), 1), depth)
    keep_up = cell < depth - 1
    keep_down = cell > 0

    def col_next(x):
        return pltpu.roll(x, rows - 1, 0)

    def col_prev(x):
        return pltpu.roll(x, 1, 0)

    def z_next(x):
        return jnp.where(keep_up, pltpu.roll(x, 127, 1), 0.0)

    def z_prev(x):
        return jnp.where(keep_down, pltpu.roll(x, 1, 1), 0.0)

    return col_next, col_prev, z_next, z_prev


def sweep(src, dst, low, high, finish):
    col_next, col_prev, z_next, z_prev = shifts(24, 128)

    def twists(i):
        v0, v1, v2 = src[0, i], src[1, i], src[2, i]
        h1 = (z_next(v0) - v0) - (src[2, i + 1] - v2)
        h2 = (src[1, i + 1] - v1) - (col_next(v0) - v0)
        return v0, v1, v2, h1, h2

    def row(i, carry):
        h1_before, h2_before = carry
        v0, v1, v2, h1, h2 = twists(i)
        h0 = (col_next(v2) - v2) - (z_next(v1) - v1)
        k0 = (h2 - col_prev(h2)) - (h1 - z_prev(h1))
        k1 = (h0 - z_prev(h0)) - (h2 - h2_before)
        k2 = (h1 - h1_before) - (h0 - col_prev(h0))
        finish(dst, i, (v0, v1, v2), (k0, k1, k2))
        return h1, h2

    before = twists(low - 1)
    carry = (before[3], before[4])

    def rows(t, carry):
        for k in range(GROUP):
            carry = row(low + GROUP * t + k, carry)
        return carry

    groups, rest = divmod(high - low, GROUP)
    carry = lax.fori_loop(0, groups, rows, carry)
    for k in range(rest):
        carry = row(low + GROUP * groups + k, carry)


def folded_sweep(src, dst, low, finish):
    col_next, col_prev, z_next, z_prev = shifts(24, 64)
    left = lax.broadcasted_iota(jnp.int32, (24, 128), 1) < 64

    def row_next(c, p, x):
        after = src[c, p + 1] if p < 11 else pltpu.roll(x, 64, 1)
        return jnp.where(left, after, src[c, p - 1] if p >= low else x)

    def twists(p):
        v0, v1, v2 = src[0, p], src[1, p], src[2, p]
        h1 = (z_next(v0) - v0) - (row_next(2, p, v2) - v2)
        h2 = (row_next(1, p, v1) - v1) - (col_next(v0) - v0)
        return (v0, v1, v2), h1, h2

    before, now = twists(low - 1), twists(low)
    for p in range(low, 12):
        values, h1, h2 = now
        if p < 11:
            after = twists(p + 1)
        else:
            after = (None, pltpu.roll(h1, 64, 1), pltpu.roll(h2, 64, 1))
        v0, v1, v2 = values
        h0 = (col_next(v2) - v2) - (z_next(v1) - v1)
        k0 = (h2 - col_prev(h2)) - (h1 - z_prev(h1))
        k1 = (h0 - z_prev(h0)) - (h2 - jnp.where(left, before[2], after[2]))
        k2 = (h1 - jnp.where(left, before[1], after[1])) - (h0 - col_prev(h0))
        finish(dst, p, values, (k0, k1, k2))
        before, now = now, after


def restrict(read, comps, sums):
    for half in range(2):
        for c in range(comps):
            for k in range(4):
                i = 2 * (7 - k if half else k)
                sums[half, c, k] = (read(c, i, 0) + read(c, i, 1)) + (read(c, i + 1, 0) + read(c, i + 1, 1))
    z = lax.broadcasted_iota(jnp.int32, (128, 128), 0)
    lane = lax.broadcasted_iota(jnp.int32, (128, 128), 1)
    total = 0.0
    for half in range(2):
        pick = jnp.where(lane == z // 2 + 64 * half, 0.125, 0.0).astype(F32)
        x = sums[half, 0:comps].reshape(comps * 32, 128)
        total = total + jnp.dot(x, pick, precision=HIGHEST, preferred_element_type=F32)
    return total.reshape(comps, 4, 8, 128)


def kernel(
    state, wave, cond, layer, mask, out,
    w, v, near, far, lay, msk, sums, ck, exa, exb, rs, rs_next, ps, arrived, zs, zarr, c0, c1, ckf, acc,
    in_sem, fine_send, fine_recv, ck_send, ck_recv, a_send, a_recv, b_send, b_recv, rs_send, rs_recv, p_send, p_recv,
    z_send, z_recv, linked,
):
    n, gx, gy = lax.axis_index("tm"), lax.axis_index("gx"), lax.axis_index("gy")
    slices = 16

    plane, column = n // 4, lax.rem(n, 4)

    def beside(di, dj):
        return (n, gx + di, gy + dj)

    def exists(di, dj):
        return (gx + di >= 0) & (gx + di < 4) & (gy + dj >= 0) & (gy + dj < 4)

    def along(planes, columns):
        return (4 * lax.rem(plane + planes + 4, 4) + lax.rem(column + columns + 4, 4), gx, gy)

    def remote(src, dst, ssem, rsem, device):
        return pltpu.make_async_remote_copy(
            src_ref=src, dst_ref=dst, send_sem=ssem, recv_sem=rsem, device_id=device, device_id_type=MESH
        )

    loads = [
        pltpu.make_async_copy(state.at[0], w.at[0:3, 4:20, 0:16], in_sem.at[0]),
        pltpu.make_async_copy(layer, lay, in_sem.at[1]),
        pltpu.make_async_copy(mask, msk, in_sem.at[2]),
    ]
    for load in loads:
        load.start()

    barrier = pltpu.get_barrier_semaphore()
    for di, dj in DIRS:

        @pl.when(exists(di, dj))
        def _(di=di, dj=dj):
            pl.semaphore_signal(barrier, inc=1, device_id=beside(di, dj), device_id_type=MESH)

    for planes, columns in ((1, 0), (2, 0), (3, 0), (0, 1), (0, 3)):
        pl.semaphore_signal(barrier, inc=1, device_id=along(planes, columns), device_id_type=MESH)

    @pl.when(gx == 0)
    def _():
        for buf in (ck, exa, exb):
            buf[0] = jnp.zeros(buf.shape[1:], F32)

    @pl.when(gx == 3)
    def _():
        for buf in (ck, exa, exb):
            buf[2] = jnp.zeros(buf.shape[1:], F32)

    @pl.when(gy == 0)
    def _():
        for buf in (ck, exa, exb):
            buf[:, 0] = jnp.zeros((3,) + buf.shape[2:], F32)
        far[1] = jnp.zeros(far.shape[1:], F32)

    @pl.when(gy == 3)
    def _():
        for buf in (ck, exa, exb):
            buf[:, 2] = jnp.zeros((3,) + buf.shape[2:], F32)
        far[0] = jnp.zeros(far.shape[1:], F32)

    for load in loads:
        load.wait()

    for i in range(16):
        chosen = jnp.full((16, 128), cond[0], F32)
        for level in range(1, 16):
            chosen = jnp.where(lay[i] == level, cond[level], chosen)
        scaled = DT / chosen
        w[3, 4 + i, 0:16] = scaled
        w[4, 4 + i, 0:16] = scaled * msk[i].astype(F32)
    near[0] = w[:, 4:20, 0:4]
    near[1] = w[:, 4:20, 12:16]

    two, three = jnp.int32(2), jnp.int32(3)
    in_x = jnp.where((gx == 0) | (gx == 3), two, three)
    in_y = jnp.where((gy == 0) | (gy == 3), two, three)
    pl.semaphore_wait(barrier, in_x * in_y - 1 + 5)
    pl.semaphore_signal(linked.at[0], inc=1, device_id=along(0, 1), device_id_type=MESH)
    pl.semaphore_signal(linked.at[1], inc=1, device_id=along(0, 3), device_id_type=MESH)

    def fine_ends(di, dj):
        if dj == 0:
            return (w.at[:, 4:8, 0:16], w.at[:, 20:24, 0:16]) if di < 0 else (w.at[:, 16:20, 0:16], w.at[:, 0:4, 0:16])
        side = 0 if dj < 0 else 1
        if di == 0:
            return near.at[side], far.at[side, :, 4:20]
        if di < 0:
            return near.at[side, :, 0:4], far.at[side, :, 20:24]
        return near.at[side, :, 12:16], far.at[side, :, 0:4]

    def swap(ends, ssem, rsem):
        copies = []
        for k, (di, dj) in enumerate(DIRS):
            source, target = ends(di, dj)
            copies.append((remote(source, target, ssem.at[k], rsem.at[k], beside(di, dj)), di, dj))

        def start():
            for copy, di, dj in copies:
                pl.when(exists(di, dj))(copy.start)

        def finish():
            for copy, di, dj in copies:
                pl.when(exists(-di, -dj))(copy.wait_recv)
            for copy, di, dj in copies:
                pl.when(exists(di, dj))(copy.wait_send)

        return start, finish

    def exchange(buf, ssem, rsem):
        return swap(lambda di, dj: (buf.at[1, 1], buf.at[1 - di, 1 - dj]), ssem, rsem)

    fine_start, fine_arrive = swap(fine_ends, fine_send, fine_recv)
    fine_start()
    ck[1, 1] = restrict(lambda c, i, b: w[3, 4 + i, pl.ds(b, 8, stride=2)], 1, sums)[0]
    ck_start, ck_arrive = exchange(ck, ck_send, ck_recv)
    ck_start()
    rs[...] = restrict(lambda c, i, b: w[c, 4 + i, pl.ds(b, 8, stride=2)], 3, sums)
    rs_copy = remote(rs, rs_next, rs_send.at[0], rs_recv.at[0], (lax.rem(n + slices - 1, slices), gx, gy))
    pl.semaphore_wait(linked.at[0], 1)
    pl.semaphore_signal(linked.at[2], inc=1, device_id=along(0, 1), device_id_type=MESH)
    pl.when(n > 0)(rs_copy.start)

    fine_arrive()
    for c in range(5):
        w[c, :, 16:20] = far[0, c]
        w[c, :, 20:24] = far[1, c]

    @pl.when(gx == 0)
    def _():
        w[:, 0:4] = jnp.zeros((5, 4, 24, 128), F32)

    @pl.when(gx == 3)
    def _():
        w[:, 20:24] = jnp.zeros((5, 4, 24, 128), F32)

    for step in range(4):
        pulse = wave[0, step]

        def finish(dst, i, values, curls, pulse=pulse):
            scaled = w[3, i]
            dst[0, i] = values[0] - scaled * curls[0] - pulse * w[4, i]
            dst[1, i] = values[1] - scaled * curls[1]
            dst[2, i] = values[2] - scaled * curls[2]

        src, dst = (w, v) if step % 2 == 0 else (v, w)
        sweep(src, dst, 1 + step, 23 - step, finish)

    end = restrict(lambda c, i, b: w[c, 4 + i, pl.ds(b, 8, stride=2)], 3, sums)
    pl.when(n < slices - 1)(rs_copy.wait_recv)
    pl.when(n > 0)(rs_copy.wait_send)
    exa[1, 1] = end - rs_next[...]
    a_start, a_arrive = exchange(exa, a_send, a_recv)
    a_start()
    b_start, b_arrive = exchange(exb, b_send, b_recv)

    left_half = lax.broadcasted_iota(jnp.int32, (8, 128), 1) < 64

    def fold(read, put):
        for tile, ej in enumerate((0, 1, -1)):
            for k in range(4):
                up, down = read(-1, ej, k), read(1, ej, k)
                put(k, tile, jnp.where(left_half, up, down))
                put(7 - k, tile, pltpu.roll(jnp.where(left_half, down, up), 64, 1))
                put(8 + k, tile, read(0, ej, k))

    ck_arrive()
    def put_kappa(row, tile, block):
        ckf[row, 8 * tile : 8 * tile + 8] = block

    fold(lambda ei, ej, k: ck[ei + 1, ej + 1, k], put_kappa)

    def unpack(buf):
        for c in range(3):

            def put(row, tile, block, c=c):
                c0[c, row, 8 * tile : 8 * tile + 8] = block

            fold(lambda ei, ej, k, c=c: buf[ei + 1, ej + 1, c, k], put)

    def finish_coarse(dst, i, values, curls):
        scaled = ckf[i]
        for c in range(3):
            dst[c, i] = values[c] - scaled * curls[c]

    def carried(b):
        return jnp.where(column + b >= 4, jnp.int32(1), jnp.int32(0))

    def power(m):
        if m > 8:
            target = (lax.rem(n + m, slices), gx, gy)
            copy = remote(ps.at[m - 1], arrived.at[m - 1], p_send.at[m - 1], p_recv.at[m - 1], target)
            return copy, n + m < slices, n - m >= 0
        planes = m // 4 + carried(m % 4)
        copy = remote(ps.at[m - 1], arrived.at[m - 1], p_send.at[m - 1], p_recv.at[m - 1], along(planes, 0))
        sent = (planes > 0) & (plane + planes < 4)
        received = (planes > 0) & (plane - planes >= 0)
        return copy, sent, received

    def one(src, dst, local, m):
        folded_sweep(src, dst, local, finish_coarse)
        ps[m - 1] = dst[:, 8:12, 0:8]

        copy, sent, _ = power(m)
        pl.when(sent)(copy.start)

    def phase(first):
        for step in range(1, 9):
            if first + step < slices:
                src, dst = (c0, c1) if step % 2 else (c1, c0)
                one(src, dst, step, first + step)

    a_arrive()
    pl.semaphore_wait(linked.at[1], 1)
    pl.semaphore_wait(linked.at[2], 1)
    unpack(exa)
    phase(0)

    @pl.when(n < slices - 9)
    def _():
        exb[1, 1] = ps[7]
        b_start()

    def across(b):
        return remote(zs.at[b - 1], zarr.at[b - 1], z_send.at[b - 1], z_recv.at[b - 1], along(0, b))

    for b in (1, 2, 3):
        kept = plane >= carried(b)

        @pl.when(carried(b) == 0)
        def _(b=b):
            zs[b - 1] = ps[b - 1]

        @pl.when(carried(b) == 1)
        def _(b=b):
            zs[b - 1] = jnp.zeros(zs.shape[1:], F32)

        for m in (b, b + 4):
            copy, _, received = power(m)

            @pl.when(received)
            def _(copy=copy, m=m, b=b):
                copy.wait_recv()
                zs[b - 1] += arrived[m - 1]

        pl.when(kept)(across(b).start)

    @pl.when(n < slices - 9)
    def _():
        b_arrive()
        unpack(exb)
        phase(8)

    acc[...] = jnp.zeros_like(acc)
    for b in (1, 2, 3):
        @pl.when((column >= b) | (plane > 0))
        def _(b=b):
            across(b).wait_recv()
            acc[...] += zarr[b - 1]

    for m in (4, 8, 9, 10, 11, 12, 13, 14, 15):
        copy, _, received = power(m)

        @pl.when(received)
        def _(copy=copy, m=m):
            copy.wait_recv()
            acc[...] += arrived[m - 1]

    for m in range(1, slices):
        copy, sent, _ = power(m)
        pl.when(sent)(copy.wait_send)
    for b in (1, 2, 3):
        pl.when(plane >= carried(b))(across(b).wait_send)

    z = lax.broadcasted_iota(jnp.int32, (128, 128), 1)
    lane = lax.broadcasted_iota(jnp.int32, (128, 128), 0)
    packed = acc[...].reshape(96, 128)
    for half in range(2):
        pick = jnp.where(lane == z // 2 + 64 * half, 1.0, 0.0).astype(F32)
        wide = jnp.dot(packed, pick, precision=HIGHEST, preferred_element_type=F32).reshape(3, 4, 8, 128)
        for c in range(3):
            for k in range(4):
                for a in range(2):
                    i = 2 * (7 - k if half else k) + a
                    for b in range(2):
                        cells = pl.ds(b, 8, stride=2)
                        out[0, c, i, cells] = w[c, 4 + i, cells] + wide[c, k]


def body(state, waveform, conductivity, layer_map, loop_mask):
    any_space = pl.BlockSpec(memory_space=pl.ANY)
    smem = pl.BlockSpec(memory_space=pltpu.SMEM)
    vmem = lambda *shape: pltpu.VMEM(shape, F32)
    dma = lambda count: pltpu.SemaphoreType.DMA((count,))
    return pl.pallas_call(
        kernel,
        out_shape=jax.ShapeDtypeStruct(state.shape, F32),
        in_specs=[any_space, smem, smem, any_space, any_space],
        out_specs=pl.BlockSpec(memory_space=pltpu.VMEM),
        scratch_shapes=[
            vmem(5, 24, 24, 128),
            vmem(3, 24, 24, 128),
            vmem(2, 5, 16, 4, 128),
            vmem(2, 5, 24, 4, 128),
            pltpu.VMEM((16, 16, 128), jnp.int32),
            pltpu.VMEM((16, 16, 128), jnp.int32),
            vmem(2, 3, 4, 8, 128),
            vmem(3, 3, 4, 8, 128),
            vmem(3, 3, 3, 4, 8, 128),
            vmem(3, 3, 3, 4, 8, 128),
            vmem(3, 4, 8, 128),
            vmem(3, 4, 8, 128),
            vmem(16, 3, 4, 8, 128),
            vmem(16, 3, 4, 8, 128),
            vmem(3, 3, 4, 8, 128),
            vmem(3, 3, 4, 8, 128),
            vmem(3, 12, 24, 128),
            vmem(3, 12, 24, 128),
            vmem(12, 24, 128),
            vmem(3, 4, 8, 128),
            dma(3),
            dma(8), dma(8), dma(8), dma(8), dma(8), dma(8), dma(8), dma(8),
            dma(1), dma(1), dma(16), dma(16), dma(3), dma(3), pltpu.SemaphoreType.REGULAR((3,)),
        ],
        compiler_params=pltpu.CompilerParams(
            collective_id=0, has_side_effects=True, vmem_limit_bytes=60 * 1024 * 1024
        ),
        name="parareal",
    )(state, waveform, conductivity, layer_map, loop_mask)


def solution(mesh):
    placed = (
        P("tm", None, "gx", "gy", None),
        P("tm", None),
        P(),
        P("gx", "gy", None),
        P("gx", "gy", None),
    )
    return jax.shard_map(
        body, mesh=mesh, in_specs=placed, out_specs=P("tm", None, "gx", "gy", None), check_vma=False
    )
```

```python
import jax
import jax.numpy as jnp
from jax import lax
from jax.experimental import pallas as pl
from jax.experimental.pallas import tpu as pltpu
from jax.sharding import PartitionSpec as P

DT = 0.015
GROUP = 8
MESH = pl.DeviceIdType.MESH
HIGHEST = lax.Precision.HIGHEST
DIRS = [(-1, 0), (1, 0), (-1, -1), (1, 1), (-1, 1), (1, -1), (0, -1), (0, 1)]
F32 = jnp.float32


def shifts(rows, depth):
    cell = lax.rem(lax.broadcasted_iota(jnp.int32, (rows, 128), 1), depth)
    keep_up = cell < depth - 1
    keep_down = cell > 0

    def col_next(x):
        return pltpu.roll(x, rows - 1, 0)

    def col_prev(x):
        return pltpu.roll(x, 1, 0)

    def z_next(x):
        return jnp.where(keep_up, pltpu.roll(x, 127, 1), 0.0)

    def z_prev(x):
        return jnp.where(keep_down, pltpu.roll(x, 1, 1), 0.0)

    return col_next, col_prev, z_next, z_prev


def sweep(src, dst, low, high, finish):
    col_next, col_prev, z_next, z_prev = shifts(24, 128)

    def twists(i):
        v0, v1, v2 = src[0, i], src[1, i], src[2, i]
        h1 = (z_next(v0) - v0) - (src[2, i + 1] - v2)
        h2 = (src[1, i + 1] - v1) - (col_next(v0) - v0)
        return v0, v1, v2, h1, h2

    def row(i, carry):
        h1_before, h2_before = carry
        v0, v1, v2, h1, h2 = twists(i)
        h0 = (col_next(v2) - v2) - (z_next(v1) - v1)
        k0 = (h2 - col_prev(h2)) - (h1 - z_prev(h1))
        k1 = (h0 - z_prev(h0)) - (h2 - h2_before)
        k2 = (h1 - h1_before) - (h0 - col_prev(h0))
        finish(dst, i, (v0, v1, v2), (k0, k1, k2))
        return h1, h2

    before = twists(low - 1)
    carry = (before[3], before[4])

    def rows(t, carry):
        for k in range(GROUP):
            carry = row(low + GROUP * t + k, carry)
        return carry

    groups, rest = divmod(high - low, GROUP)
    carry = lax.fori_loop(0, groups, rows, carry)
    for k in range(rest):
        carry = row(low + GROUP * groups + k, carry)


def folded_sweep(src, dst, low, finish):
    col_next, col_prev, z_next, z_prev = shifts(24, 64)
    left = lax.broadcasted_iota(jnp.int32, (24, 128), 1) < 64

    def row_next(c, p, x):
        after = src[c, p + 1] if p < 11 else pltpu.roll(x, 64, 1)
        return jnp.where(left, after, src[c, p - 1] if p >= low else x)

    def twists(p):
        v0, v1, v2 = src[0, p], src[1, p], src[2, p]
        h1 = (z_next(v0) - v0) - (row_next(2, p, v2) - v2)
        h2 = (row_next(1, p, v1) - v1) - (col_next(v0) - v0)
        return (v0, v1, v2), h1, h2

    before, now = twists(low - 1), twists(low)
    for p in range(low, 12):
        values, h1, h2 = now
        if p < 11:
            after = twists(p + 1)
        else:
            after = (None, pltpu.roll(h1, 64, 1), pltpu.roll(h2, 64, 1))
        v0, v1, v2 = values
        h0 = (col_next(v2) - v2) - (z_next(v1) - v1)
        k0 = (h2 - col_prev(h2)) - (h1 - z_prev(h1))
        k1 = (h0 - z_prev(h0)) - (h2 - jnp.where(left, before[2], after[2]))
        k2 = (h1 - jnp.where(left, before[1], after[1])) - (h0 - col_prev(h0))
        finish(dst, p, values, (k0, k1, k2))
        before, now = now, after


def restrict(read, comps, sums):
    for half in range(2):
        for c in range(comps):
            for k in range(4):
                i = 2 * (7 - k if half else k)
                sums[half, c, k] = (read(c, i, 0) + read(c, i, 1)) + (read(c, i + 1, 0) + read(c, i + 1, 1))
    z = lax.broadcasted_iota(jnp.int32, (128, 128), 0)
    lane = lax.broadcasted_iota(jnp.int32, (128, 128), 1)
    total = 0.0
    for half in range(2):
        pick = jnp.where(lane == z // 2 + 64 * half, 0.125, 0.0).astype(F32)
        x = sums[half, 0:comps].reshape(comps * 32, 128)
        total = total + jnp.dot(x, pick, precision=HIGHEST, preferred_element_type=F32)
    return total.reshape(comps, 4, 8, 128)


def kernel(
    state, wave, cond, layer, mask, out,
    w, v, near, far, lay, msk, sums, ck, exa, exb, rs, rs_next, ps, arrived, zs, zarr, c0, c1, ckf, acc,
    in_sem, fine_send, fine_recv, ck_send, ck_recv, a_send, a_recv, b_send, b_recv, rs_send, rs_recv, p_send, p_recv,
    z_send, z_recv, answers, whole,
):
    n, gx, gy = lax.axis_index("tm"), lax.axis_index("gx"), lax.axis_index("gy")
    slices = 16

    plane, column = n // 4, lax.rem(n, 4)

    def beside(di, dj):
        return (n, gx + di, gy + dj)

    def exists(di, dj):
        return (gx + di >= 0) & (gx + di < 4) & (gy + dj >= 0) & (gy + dj < 4)

    def along(planes, columns):
        return (4 * lax.rem(plane + planes + 4, 4) + lax.rem(column + columns + 4, 4), gx, gy)

    def remote(src, dst, ssem, rsem, device):
        return pltpu.make_async_remote_copy(
            src_ref=src, dst_ref=dst, send_sem=ssem, recv_sem=rsem, device_id=device, device_id_type=MESH
        )

    barrier = pltpu.get_barrier_semaphore()
    for step in (1, 2, 3):

        @pl.when(column + step < 4)
        def _(step=step):
            pl.semaphore_signal(barrier, inc=1, device_id=along(0, step), device_id_type=MESH)

        @pl.when(plane + step < 4)
        def _(step=step):
            pl.semaphore_signal(barrier, inc=1, device_id=along(step, 0), device_id_type=MESH)

    for di, dj in DIRS:

        @pl.when(exists(di, dj))
        def _(di=di, dj=dj):
            pl.semaphore_signal(barrier, inc=1, device_id=beside(di, dj), device_id_type=MESH)

    loads = [
        pltpu.make_async_copy(state.at[0], w.at[0:3, 4:20, 0:16], in_sem.at[0]),
        pltpu.make_async_copy(layer, lay, in_sem.at[1]),
        pltpu.make_async_copy(mask, msk, in_sem.at[2]),
    ]
    for load in loads:
        load.start()

    @pl.when(gx == 0)
    def _():
        for buf in (ck, exa, exb):
            buf[0] = jnp.zeros(buf.shape[1:], F32)

    @pl.when(gx == 3)
    def _():
        for buf in (ck, exa, exb):
            buf[2] = jnp.zeros(buf.shape[1:], F32)

    @pl.when(gy == 0)
    def _():
        for buf in (ck, exa, exb):
            buf[:, 0] = jnp.zeros((3,) + buf.shape[2:], F32)
        far[1] = jnp.zeros(far.shape[1:], F32)

    @pl.when(gy == 3)
    def _():
        for buf in (ck, exa, exb):
            buf[:, 2] = jnp.zeros((3,) + buf.shape[2:], F32)
        far[0] = jnp.zeros(far.shape[1:], F32)

    for load in loads:
        load.wait()

    for i in range(16):
        chosen = jnp.full((16, 128), cond[0], F32)
        for level in range(1, 16):
            chosen = jnp.where(lay[i] == level, cond[level], chosen)
        scaled = DT / chosen
        w[3, 4 + i, 0:16] = scaled
        w[4, 4 + i, 0:16] = scaled * msk[i].astype(F32)
    near[0] = w[:, 4:20, 0:4]
    near[1] = w[:, 4:20, 12:16]

    two, three = jnp.int32(2), jnp.int32(3)
    in_x = jnp.where((gx == 0) | (gx == 3), two, three)
    in_y = jnp.where((gy == 0) | (gy == 3), two, three)
    pl.semaphore_wait(barrier, in_x * in_y - 1 + plane + column)

    def fine_ends(di, dj):
        if dj == 0:
            return (w.at[:, 4:8, 0:16], w.at[:, 20:24, 0:16]) if di < 0 else (w.at[:, 16:20, 0:16], w.at[:, 0:4, 0:16])
        side = 0 if dj < 0 else 1
        if di == 0:
            return near.at[side], far.at[side, :, 4:20]
        if di < 0:
            return near.at[side, :, 0:4], far.at[side, :, 20:24]
        return near.at[side, :, 12:16], far.at[side, :, 0:4]

    def swap(ends, ssem, rsem):
        copies = []
        for k, (di, dj) in enumerate(DIRS):
            source, target = ends(di, dj)
            copies.append((remote(source, target, ssem.at[k], rsem.at[k], beside(di, dj)), di, dj))

        def start():
            for copy, di, dj in copies:
                pl.when(exists(di, dj))(copy.start)

        def finish():
            for copy, di, dj in copies:
                pl.when(exists(-di, -dj))(copy.wait_recv)
            for copy, di, dj in copies:
                pl.when(exists(di, dj))(copy.wait_send)

        return start, finish

    def exchange(buf, ssem, rsem):
        return swap(lambda di, dj: (buf.at[1, 1], buf.at[1 - di, 1 - dj]), ssem, rsem)

    fine_start, fine_arrive = swap(fine_ends, fine_send, fine_recv)
    fine_start()
    for step in (1, 2, 3):

        @pl.when(column - step >= 0)
        def _(step=step):
            pl.semaphore_signal(answers.at[step - 1], inc=1, device_id=along(0, -step), device_id_type=MESH)

        @pl.when(plane - step >= 0)
        def _(step=step):
            pl.semaphore_signal(answers.at[3], inc=1, device_id=along(-step, 0), device_id_type=MESH)

    ck[1, 1] = restrict(lambda c, i, b: w[3, 4 + i, pl.ds(b, 8, stride=2)], 1, sums)[0]
    ck_start, ck_arrive = exchange(ck, ck_send, ck_recv)
    ck_start()
    rs[...] = restrict(lambda c, i, b: w[c, 4 + i, pl.ds(b, 8, stride=2)], 3, sums)
    rs_copy = remote(rs, rs_next, rs_send.at[0], rs_recv.at[0], (lax.rem(n + slices - 1, slices), gx, gy))
    pl.when(column > 0)(rs_copy.start)

    fine_arrive()
    for c in range(5):
        w[c, :, 16:20] = far[0, c]
        w[c, :, 20:24] = far[1, c]

    @pl.when(gx == 0)
    def _():
        w[:, 0:4] = jnp.zeros((5, 4, 24, 128), F32)

    @pl.when(gx == 3)
    def _():
        w[:, 20:24] = jnp.zeros((5, 4, 24, 128), F32)

    for step in range(4):
        pulse = wave[0, step]

        def finish(dst, i, values, curls, pulse=pulse):
            scaled = w[3, i]
            dst[0, i] = values[0] - scaled * curls[0] - pulse * w[4, i]
            dst[1, i] = values[1] - scaled * curls[1]
            dst[2, i] = values[2] - scaled * curls[2]

        src, dst = (w, v) if step % 2 == 0 else (v, w)
        sweep(src, dst, 1 + step, 23 - step, finish)

    end = restrict(lambda c, i, b: w[c, 4 + i, pl.ds(b, 8, stride=2)], 3, sums)
    @pl.when(column == 0)
    def _():
        pl.semaphore_wait(answers.at[2], 1)

    pl.when((column == 0) & (n > 0))(rs_copy.start)
    pl.when(n < slices - 1)(rs_copy.wait_recv)
    pl.when(n > 0)(rs_copy.wait_send)
    exa[1, 1] = end - rs_next[...]
    a_start, a_arrive = exchange(exa, a_send, a_recv)
    a_start()
    for step in (1, 2):

        @pl.when(column + step < 4)
        def _(step=step):
            pl.semaphore_wait(answers.at[step - 1], 1)

    @pl.when(plane < 3)
    def _():
        pl.semaphore_wait(answers.at[3], 3 - plane)

    for step in (1, 2, 3):
        pl.semaphore_signal(whole, inc=1, device_id=along(0, step), device_id_type=MESH)
    b_start, b_arrive = exchange(exb, b_send, b_recv)

    left_half = lax.broadcasted_iota(jnp.int32, (8, 128), 1) < 64

    def fold(read, put):
        for tile, ej in enumerate((0, 1, -1)):
            for k in range(4):
                up, down = read(-1, ej, k), read(1, ej, k)
                put(k, tile, jnp.where(left_half, up, down))
                put(7 - k, tile, pltpu.roll(jnp.where(left_half, down, up), 64, 1))
                put(8 + k, tile, read(0, ej, k))

    ck_arrive()
    def put_kappa(row, tile, block):
        ckf[row, 8 * tile : 8 * tile + 8] = block

    fold(lambda ei, ej, k: ck[ei + 1, ej + 1, k], put_kappa)

    def unpack(buf):
        for c in range(3):

            def put(row, tile, block, c=c):
                c0[c, row, 8 * tile : 8 * tile + 8] = block

            fold(lambda ei, ej, k, c=c: buf[ei + 1, ej + 1, c, k], put)

    def finish_coarse(dst, i, values, curls):
        scaled = ckf[i]
        for c in range(3):
            dst[c, i] = values[c] - scaled * curls[c]

    def carried(b):
        return jnp.where(column + b >= 4, jnp.int32(1), jnp.int32(0))

    def power(m):
        if m > 8:
            target = (lax.rem(n + m, slices), gx, gy)
            copy = remote(ps.at[m - 1], arrived.at[m - 1], p_send.at[m - 1], p_recv.at[m - 1], target)
            return copy, n + m < slices, n - m >= 0
        planes = m // 4 + carried(m % 4)
        copy = remote(ps.at[m - 1], arrived.at[m - 1], p_send.at[m - 1], p_recv.at[m - 1], along(planes, 0))
        sent = (planes > 0) & (plane + planes < 4)
        received = (planes > 0) & (plane - planes >= 0)
        return copy, sent, received

    def one(src, dst, local, m):
        folded_sweep(src, dst, local, finish_coarse)
        ps[m - 1] = dst[:, 8:12, 0:8]

        copy, sent, _ = power(m)
        pl.when(sent)(copy.start)

    def phase(first):
        for step in range(1, 9):
            if first + step < slices:
                src, dst = (c0, c1) if step % 2 else (c1, c0)
                one(src, dst, step, first + step)

    a_arrive()
    unpack(exa)
    phase(0)

    @pl.when(n < slices - 9)
    def _():
        exb[1, 1] = ps[7]
        b_start()

    def across(b):
        return remote(zs.at[b - 1], zarr.at[b - 1], z_send.at[b - 1], z_recv.at[b - 1], along(0, b))

    for b in (1, 2, 3):
        kept = plane >= carried(b)

        @pl.when(carried(b) == 0)
        def _(b=b):
            zs[b - 1] = ps[b - 1]

        @pl.when(carried(b) == 1)
        def _(b=b):
            zs[b - 1] = jnp.zeros(zs.shape[1:], F32)

        for m in (b, b + 4):
            copy, _, received = power(m)

            @pl.when(received)
            def _(copy=copy, m=m, b=b):
                copy.wait_recv()
                zs[b - 1] += arrived[m - 1]

        pl.when(kept)(across(b).start)

    pl.semaphore_wait(whole, 3)

    @pl.when(n < slices - 9)
    def _():
        b_arrive()
        unpack(exb)
        phase(8)

    acc[...] = jnp.zeros_like(acc)
    for b in (1, 2, 3):
        @pl.when((column >= b) | (plane > 0))
        def _(b=b):
            across(b).wait_recv()
            acc[...] += zarr[b - 1]

    for m in (4, 8, 9, 10, 11, 12, 13, 14, 15):
        copy, _, received = power(m)

        @pl.when(received)
        def _(copy=copy, m=m):
            copy.wait_recv()
            acc[...] += arrived[m - 1]

    for m in range(1, slices):
        copy, sent, _ = power(m)
        pl.when(sent)(copy.wait_send)
    for b in (1, 2, 3):
        pl.when(plane >= carried(b))(across(b).wait_send)

    z = lax.broadcasted_iota(jnp.int32, (128, 128), 1)
    lane = lax.broadcasted_iota(jnp.int32, (128, 128), 0)
    packed = acc[...].reshape(96, 128)
    for half in range(2):
        pick = jnp.where(lane == z // 2 + 64 * half, 1.0, 0.0).astype(F32)
        wide = jnp.dot(packed, pick, precision=HIGHEST, preferred_element_type=F32).reshape(3, 4, 8, 128)
        for c in range(3):
            for k in range(4):
                for a in range(2):
                    i = 2 * (7 - k if half else k) + a
                    for b in range(2):
                        cells = pl.ds(b, 8, stride=2)
                        out[0, c, i, cells] = w[c, 4 + i, cells] + wide[c, k]


def body(state, waveform, conductivity, layer_map, loop_mask):
    any_space = pl.BlockSpec(memory_space=pl.ANY)
    smem = pl.BlockSpec(memory_space=pltpu.SMEM)
    vmem = lambda *shape: pltpu.VMEM(shape, F32)
    dma = lambda count: pltpu.SemaphoreType.DMA((count,))
    return pl.pallas_call(
        kernel,
        out_shape=jax.ShapeDtypeStruct(state.shape, F32),
        in_specs=[any_space, smem, smem, any_space, any_space],
        out_specs=pl.BlockSpec(memory_space=pltpu.VMEM),
        scratch_shapes=[
            vmem(5, 24, 24, 128),
            vmem(3, 24, 24, 128),
            vmem(2, 5, 16, 4, 128),
            vmem(2, 5, 24, 4, 128),
            pltpu.VMEM((16, 16, 128), jnp.int32),
            pltpu.VMEM((16, 16, 128), jnp.int32),
            vmem(2, 3, 4, 8, 128),
            vmem(3, 3, 4, 8, 128),
            vmem(3, 3, 3, 4, 8, 128),
            vmem(3, 3, 3, 4, 8, 128),
            vmem(3, 4, 8, 128),
            vmem(3, 4, 8, 128),
            vmem(16, 3, 4, 8, 128),
            vmem(16, 3, 4, 8, 128),
            vmem(3, 3, 4, 8, 128),
            vmem(3, 3, 4, 8, 128),
            vmem(3, 12, 24, 128),
            vmem(3, 12, 24, 128),
            vmem(12, 24, 128),
            vmem(3, 4, 8, 128),
            dma(3),
            dma(8), dma(8), dma(8), dma(8), dma(8), dma(8), dma(8), dma(8),
            dma(1), dma(1), dma(16), dma(16), dma(3), dma(3), pltpu.SemaphoreType.REGULAR((4,)), pltpu.SemaphoreType.REGULAR,
        ],
        compiler_params=pltpu.CompilerParams(
            collective_id=0, has_side_effects=True, vmem_limit_bytes=60 * 1024 * 1024
        ),
        name="parareal",
    )(state, waveform, conductivity, layer_map, loop_mask)


def solution(mesh):
    placed = (
        P("tm", None, "gx", "gy", None),
        P("tm", None),
        P(),
        P("gx", "gy", None),
        P("gx", "gy", None),
    )
    return jax.shard_map(
        body, mesh=mesh, in_specs=placed, out_specs=P("tm", None, "gx", "gy", None), check_vma=False
    )
```

```python
import jax
import jax.numpy as jnp
from jax import lax
from jax.experimental import pallas as pl
from jax.experimental.pallas import tpu as pltpu
from jax.sharding import PartitionSpec as P

DT = 0.015
GROUP = 8
DIRECT = (9, 10, 11, 12, 13, 14, 15)
MESH = pl.DeviceIdType.MESH
HIGHEST = lax.Precision.HIGHEST
DIRS = [(-1, 0), (1, 0), (-1, -1), (1, 1), (-1, 1), (1, -1), (0, -1), (0, 1)]
F32 = jnp.float32


def shifts(rows, depth):
    cell = lax.rem(lax.broadcasted_iota(jnp.int32, (rows, 128), 1), depth)
    keep_up = cell < depth - 1
    keep_down = cell > 0

    def col_next(x):
        return pltpu.roll(x, rows - 1, 0)

    def col_prev(x):
        return pltpu.roll(x, 1, 0)

    def z_next(x):
        return jnp.where(keep_up, pltpu.roll(x, 127, 1), 0.0)

    def z_prev(x):
        return jnp.where(keep_down, pltpu.roll(x, 1, 1), 0.0)

    return col_next, col_prev, z_next, z_prev


def sweep(src, dst, low, high, finish):
    col_next, col_prev, z_next, z_prev = shifts(24, 128)

    def twists(i):
        v0, v1, v2 = src[0, i], src[1, i], src[2, i]
        h1 = (z_next(v0) - v0) - (src[2, i + 1] - v2)
        h2 = (src[1, i + 1] - v1) - (col_next(v0) - v0)
        return v0, v1, v2, h1, h2

    def row(i, carry):
        h1_before, h2_before = carry
        v0, v1, v2, h1, h2 = twists(i)
        h0 = (col_next(v2) - v2) - (z_next(v1) - v1)
        k0 = (h2 - col_prev(h2)) - (h1 - z_prev(h1))
        k1 = (h0 - z_prev(h0)) - (h2 - h2_before)
        k2 = (h1 - h1_before) - (h0 - col_prev(h0))
        finish(dst, i, (v0, v1, v2), (k0, k1, k2))
        return h1, h2

    before = twists(low - 1)
    carry = (before[3], before[4])

    def rows(t, carry):
        for k in range(GROUP):
            carry = row(low + GROUP * t + k, carry)
        return carry

    groups, rest = divmod(high - low, GROUP)
    carry = lax.fori_loop(0, groups, rows, carry)
    for k in range(rest):
        carry = row(low + GROUP * groups + k, carry)


def folded_sweep(src, dst, low, finish):
    col_next, col_prev, z_next, z_prev = shifts(24, 64)
    left = lax.broadcasted_iota(jnp.int32, (24, 128), 1) < 64

    def row_next(c, p, x):
        after = src[c, p + 1] if p < 11 else pltpu.roll(x, 64, 1)
        return jnp.where(left, after, src[c, p - 1] if p >= low else x)

    def twists(p):
        v0, v1, v2 = src[0, p], src[1, p], src[2, p]
        h1 = (z_next(v0) - v0) - (row_next(2, p, v2) - v2)
        h2 = (row_next(1, p, v1) - v1) - (col_next(v0) - v0)
        return (v0, v1, v2), h1, h2

    before, now = twists(low - 1), twists(low)
    for p in range(low, 12):
        values, h1, h2 = now
        if p < 11:
            after = twists(p + 1)
        else:
            after = (None, pltpu.roll(h1, 64, 1), pltpu.roll(h2, 64, 1))
        v0, v1, v2 = values
        h0 = (col_next(v2) - v2) - (z_next(v1) - v1)
        k0 = (h2 - col_prev(h2)) - (h1 - z_prev(h1))
        k1 = (h0 - z_prev(h0)) - (h2 - jnp.where(left, before[2], after[2]))
        k2 = (h1 - jnp.where(left, before[1], after[1])) - (h0 - col_prev(h0))
        finish(dst, p, values, (k0, k1, k2))
        before, now = now, after


def restrict(read, comps, sums):
    for half in range(2):
        for c in range(comps):
            for k in range(4):
                i = 2 * (7 - k if half else k)
                sums[half, c, k] = (read(c, i, 0) + read(c, i, 1)) + (read(c, i + 1, 0) + read(c, i + 1, 1))
    z = lax.broadcasted_iota(jnp.int32, (128, 128), 0)
    lane = lax.broadcasted_iota(jnp.int32, (128, 128), 1)
    total = 0.0
    for half in range(2):
        pick = jnp.where(lane == z // 2 + 64 * half, 0.125, 0.0).astype(F32)
        x = sums[half, 0:comps].reshape(comps * 32, 128)
        total = total + jnp.dot(x, pick, precision=HIGHEST, preferred_element_type=F32)
    return total.reshape(comps, 4, 8, 128)


def kernel(
    state, wave, cond, layer, mask, out,
    w, v, near, far, lay, msk, sums, ck, exs, exa, exb, ps, arrived, zs, zarr, c0, c1, lead, ckf, acc, held,
    in_sem, fine_send, fine_recv, ck_send, ck_recv, a_send, a_recv, b_send, b_recv, s_send, s_recv, p_send, p_recv,
    z_send, z_recv, answers, whole,
):
    n, gx, gy = lax.axis_index("tm"), lax.axis_index("gx"), lax.axis_index("gy")
    slices = 16

    plane, column = n // 4, lax.rem(n, 4)

    def beside(di, dj):
        return (n, gx + di, gy + dj)

    def exists(di, dj):
        return (gx + di >= 0) & (gx + di < 4) & (gy + dj >= 0) & (gy + dj < 4)

    def along(planes, columns):
        return (4 * lax.rem(plane + planes + 4, 4) + lax.rem(column + columns + 4, 4), gx, gy)

    def remote(src, dst, ssem, rsem, device):
        return pltpu.make_async_remote_copy(
            src_ref=src, dst_ref=dst, send_sem=ssem, recv_sem=rsem, device_id=device, device_id_type=MESH
        )

    barrier = pltpu.get_barrier_semaphore()
    for step in (1, 2, 3):

        @pl.when(column + step < 4)
        def _(step=step):
            pl.semaphore_signal(barrier, inc=1, device_id=along(0, step), device_id_type=MESH)

        @pl.when(plane + step < 4)
        def _(step=step):
            pl.semaphore_signal(barrier, inc=1, device_id=along(step, 0), device_id_type=MESH)

    for di, dj in DIRS:

        @pl.when(exists(di, dj))
        def _(di=di, dj=dj):
            pl.semaphore_signal(barrier, inc=1, device_id=beside(di, dj), device_id_type=MESH)

    loads = [
        pltpu.make_async_copy(state.at[0], w.at[0:3, 4:20, 0:16], in_sem.at[0]),
        pltpu.make_async_copy(layer, lay, in_sem.at[1]),
        pltpu.make_async_copy(mask, msk, in_sem.at[2]),
    ]
    for load in loads:
        load.start()

    @pl.when(gx == 0)
    def _():
        for buf in (ck, exs, exa, exb):
            buf[0] = jnp.zeros(buf.shape[1:], F32)

    @pl.when(gx == 3)
    def _():
        for buf in (ck, exs, exa, exb):
            buf[2] = jnp.zeros(buf.shape[1:], F32)

    @pl.when(gy == 0)
    def _():
        for buf in (ck, exs, exa, exb):
            buf[:, 0] = jnp.zeros((3,) + buf.shape[2:], F32)
        far[1] = jnp.zeros(far.shape[1:], F32)

    @pl.when(gy == 3)
    def _():
        for buf in (ck, exs, exa, exb):
            buf[:, 2] = jnp.zeros((3,) + buf.shape[2:], F32)
        far[0] = jnp.zeros(far.shape[1:], F32)

    for load in loads:
        load.wait()

    for i in range(16):
        chosen = jnp.full((16, 128), cond[0], F32)
        for level in range(1, 16):
            chosen = jnp.where(lay[i] == level, cond[level], chosen)
        scaled = DT / chosen
        w[3, 4 + i, 0:16] = scaled
        w[4, 4 + i, 0:16] = scaled * msk[i].astype(F32)
    near[0] = w[:, 4:20, 0:4]
    near[1] = w[:, 4:20, 12:16]

    two, three = jnp.int32(2), jnp.int32(3)
    in_x = jnp.where((gx == 0) | (gx == 3), two, three)
    in_y = jnp.where((gy == 0) | (gy == 3), two, three)
    pl.semaphore_wait(barrier, in_x * in_y - 1 + plane + column)

    def fine_ends(di, dj):
        if dj == 0:
            return (w.at[:, 4:8, 0:16], w.at[:, 20:24, 0:16]) if di < 0 else (w.at[:, 16:20, 0:16], w.at[:, 0:4, 0:16])
        side = 0 if dj < 0 else 1
        if di == 0:
            return near.at[side], far.at[side, :, 4:20]
        if di < 0:
            return near.at[side, :, 0:4], far.at[side, :, 20:24]
        return near.at[side, :, 12:16], far.at[side, :, 0:4]

    def swap(ends, ssem, rsem):
        copies = []
        for k, (di, dj) in enumerate(DIRS):
            source, target = ends(di, dj)
            copies.append((remote(source, target, ssem.at[k], rsem.at[k], beside(di, dj)), di, dj))

        def start():
            for copy, di, dj in copies:
                pl.when(exists(di, dj))(copy.start)

        def finish():
            for copy, di, dj in copies:
                pl.when(exists(-di, -dj))(copy.wait_recv)
            for copy, di, dj in copies:
                pl.when(exists(di, dj))(copy.wait_send)

        return start, finish

    def exchange(buf, ssem, rsem):
        return swap(lambda di, dj: (buf.at[1, 1], buf.at[1 - di, 1 - dj]), ssem, rsem)

    fine_start, fine_arrive = swap(fine_ends, fine_send, fine_recv)
    fine_start()
    for step in (1, 2, 3):

        @pl.when(column - step >= 0)
        def _(step=step):
            pl.semaphore_signal(answers.at[step - 1], inc=1, device_id=along(0, -step), device_id_type=MESH)

        @pl.when(plane - step >= 0)
        def _(step=step):
            pl.semaphore_signal(answers.at[3], inc=1, device_id=along(-step, 0), device_id_type=MESH)

    ck[1, 1] = restrict(lambda c, i, b: w[3, 4 + i, pl.ds(b, 8, stride=2)], 1, sums)[0]
    ck_start, ck_arrive = exchange(ck, ck_send, ck_recv)
    ck_start()
    exs[1, 1] = restrict(lambda c, i, b: w[c, 4 + i, pl.ds(b, 8, stride=2)], 3, sums)
    s_start, s_arrive = exchange(exs, s_send, s_recv)
    s_start()

    fine_arrive()
    for c in range(5):
        w[c, :, 16:20] = far[0, c]
        w[c, :, 20:24] = far[1, c]

    @pl.when(gx == 0)
    def _():
        w[:, 0:4] = jnp.zeros((5, 4, 24, 128), F32)

    @pl.when(gx == 3)
    def _():
        w[:, 20:24] = jnp.zeros((5, 4, 24, 128), F32)

    for step in range(4):
        pulse = wave[0, step]

        def finish(dst, i, values, curls, pulse=pulse):
            scaled = w[3, i]
            dst[0, i] = values[0] - scaled * curls[0] - pulse * w[4, i]
            dst[1, i] = values[1] - scaled * curls[1]
            dst[2, i] = values[2] - scaled * curls[2]

        src, dst = (w, v) if step % 2 == 0 else (v, w)
        sweep(src, dst, 1 + step, 23 - step, finish)

    end = restrict(lambda c, i, b: w[c, 4 + i, pl.ds(b, 8, stride=2)], 3, sums)
    exa[1, 1] = end
    a_start, a_arrive = exchange(exa, a_send, a_recv)
    a_start()
    for step in (1, 2, 3):

        @pl.when(column + step < 4)
        def _(step=step):
            pl.semaphore_wait(answers.at[step - 1], 1)

    @pl.when(plane < 3)
    def _():
        pl.semaphore_wait(answers.at[3], 3 - plane)

    for step in (1, 2, 3):
        pl.semaphore_signal(whole, inc=1, device_id=along(0, step), device_id_type=MESH)
    b_start, b_arrive = exchange(exb, b_send, b_recv)

    left_half = lax.broadcasted_iota(jnp.int32, (8, 128), 1) < 64

    def fold(read, put):
        for tile, ej in enumerate((0, 1, -1)):
            for k in range(4):
                up, down = read(-1, ej, k), read(1, ej, k)
                put(k, tile, jnp.where(left_half, up, down))
                put(7 - k, tile, pltpu.roll(jnp.where(left_half, down, up), 64, 1))
                put(8 + k, tile, read(0, ej, k))

    ck_arrive()
    def put_kappa(row, tile, block):
        ckf[row, 8 * tile : 8 * tile + 8] = block

    fold(lambda ei, ej, k: ck[ei + 1, ej + 1, k], put_kappa)

    def unpack(buf, less=None):
        for c in range(3):

            def put(row, tile, block, c=c):
                columns = slice(8 * tile, 8 * tile + 8)
                c0[c, row, columns] = block if less is None else block - less[c, row, columns]

            fold(lambda ei, ej, k, c=c: buf[ei + 1, ej + 1, c, k], put)

    def finish_coarse(dst, i, values, curls):
        scaled = ckf[i]
        for c in range(3):
            dst[c, i] = values[c] - scaled * curls[c]

    def carried(b):
        return jnp.where(column + b >= 4, jnp.int32(1), jnp.int32(0))

    def power(m):
        if m in DIRECT:
            target = (lax.rem(n + m, slices), gx, gy)
            copy = remote(ps.at[m - 1], arrived.at[m - 1], p_send.at[m - 1], p_recv.at[m - 1], target)
            return copy, n + m < slices, n - m >= 0
        planes = m // 4 + carried(m % 4)
        copy = remote(ps.at[m - 1], arrived.at[m - 1], p_send.at[m - 1], p_recv.at[m - 1], along(planes, 0))
        sent = (planes > 0) & (plane + planes < 4)
        received = (planes > 0) & (plane - planes >= 0)
        return copy, sent, received

    def one(src, dst, low, m):
        @pl.when(n + m < slices)
        def _():
            folded_sweep(src, dst, low, finish_coarse)
            ps[m - 1] = dst[:, 8:12, 0:8]
            copy, sent, _ = power(m)
            pl.when(sent)(copy.start)

    s_arrive()
    unpack(exs)
    folded_sweep(c0, lead, 1, finish_coarse)

    @pl.when(n == 0)
    def _():
        lead[...] = jnp.zeros_like(lead)

    a_arrive()
    pl.semaphore_wait(whole, 3)
    unpack(exa, lead)
    for m in range(1, 8):
        src, dst = (c0, c1) if m % 2 else (c1, c0)
        one(src, dst, m + 1, m)

    @pl.when(n < slices - 8)
    def _():
        exb[1, 1] = ps[6]
        b_start()

    def across(b):
        return remote(zs.at[b - 1], zarr.at[b - 1], z_send.at[b - 1], z_recv.at[b - 1], along(0, b))

    for b in (1, 2, 3):
        for m in (b, b + 4):
            if m in DIRECT:
                continue
            copy, _, received = power(m)
            first = m == b or b in DIRECT

            if m == b:

                @pl.when(carried(b) == 0)
                def _(b=b):
                    zs[b - 1] = ps[b - 1]

            @pl.when(received)
            def _(copy=copy, m=m, b=b, first=first):
                copy.wait_recv()
                if first:
                    zs[b - 1] = arrived[m - 1]
                else:
                    zs[b - 1] += arrived[m - 1]

        if b not in DIRECT:
            pl.when(plane >= carried(b))(across(b).start)
        elif b + 4 not in DIRECT:
            pl.when(plane >= 1 + carried(b))(across(b).start)

    @pl.when(n < slices - 8)
    def _():
        b_arrive()
        unpack(exb)
        for m in range(8, slices):
            src, dst = (c1, c0) if m % 2 else (c0, c1)
            one(src, dst, m - 7, m)

    acc[...] = -lead[:, 8:12, 0:8]
    for b in (1, 2, 3):
        if b in DIRECT and b + 4 in DIRECT:
            continue

        late = 1 if b in DIRECT else 0

        @pl.when(plane >= late + jnp.where(column >= b, jnp.int32(0), jnp.int32(1)))
        def _(b=b):
            across(b).wait_recv()
            acc[...] += zarr[b - 1]

    for m in sorted({4, 8, 12, *DIRECT}):
        copy, _, received = power(m)

        @pl.when(received)
        def _(copy=copy, m=m):
            copy.wait_recv()
            acc[...] += arrived[m - 1]

    z = lax.broadcasted_iota(jnp.int32, (128, 128), 1)
    lane = lax.broadcasted_iota(jnp.int32, (128, 128), 0)
    packed = acc[...].reshape(96, 128)
    wide = []
    for half in range(2):
        pick = jnp.where(lane == z // 2 + 64 * half, 1.0, 0.0).astype(F32)
        wide.append(jnp.dot(packed, pick, precision=HIGHEST, preferred_element_type=F32).reshape(3, 4, 8, 128))
    stores = []
    for c in range(3):
        for half in range(2):
            for k in range(4):
                for a in range(2):
                    i = 2 * (7 - k if half else k) + a
                    for b in range(2):
                        cells = pl.ds(b, 8, stride=2)
                        held[c, i, cells] = w[c, 4 + i, cells] + wide[half][c, k]
        stores.append(pltpu.make_async_copy(held.at[c], out.at[0, c], in_sem.at[c]))
        stores[c].start()

    for m in range(1, slices):
        copy, sent, _ = power(m)
        pl.when(sent)(copy.wait_send)
    for b in (1, 2, 3):
        if b not in DIRECT:
            pl.when(plane >= carried(b))(across(b).wait_send)
        elif b + 4 not in DIRECT:
            pl.when(plane >= 1 + carried(b))(across(b).wait_send)
    for store in stores:
        store.wait()


def body(state, waveform, conductivity, layer_map, loop_mask):
    any_space = pl.BlockSpec(memory_space=pl.ANY)
    smem = pl.BlockSpec(memory_space=pltpu.SMEM)
    vmem = lambda *shape: pltpu.VMEM(shape, F32)
    dma = lambda count: pltpu.SemaphoreType.DMA((count,))
    return pl.pallas_call(
        kernel,
        out_shape=jax.ShapeDtypeStruct(state.shape, F32),
        in_specs=[any_space, smem, smem, any_space, any_space],
        out_specs=any_space,
        scratch_shapes=[
            vmem(5, 24, 24, 128),
            vmem(3, 24, 24, 128),
            vmem(2, 5, 16, 4, 128),
            vmem(2, 5, 24, 4, 128),
            pltpu.VMEM((16, 16, 128), jnp.int32),
            pltpu.VMEM((16, 16, 128), jnp.int32),
            vmem(2, 3, 4, 8, 128),
            vmem(3, 3, 4, 8, 128),
            vmem(3, 3, 3, 4, 8, 128),
            vmem(3, 3, 3, 4, 8, 128),
            vmem(3, 3, 3, 4, 8, 128),
            vmem(16, 3, 4, 8, 128),
            vmem(16, 3, 4, 8, 128),
            vmem(3, 3, 4, 8, 128),
            vmem(3, 3, 4, 8, 128),
            vmem(3, 12, 24, 128),
            vmem(3, 12, 24, 128),
            vmem(3, 12, 24, 128),
            vmem(12, 24, 128),
            vmem(3, 4, 8, 128),
            vmem(3, 16, 16, 128),
            dma(3),
            dma(8), dma(8), dma(8), dma(8), dma(8), dma(8), dma(8), dma(8),
            dma(8), dma(8), dma(16), dma(16), dma(3), dma(3), pltpu.SemaphoreType.REGULAR((4,)), pltpu.SemaphoreType.REGULAR,
        ],
        compiler_params=pltpu.CompilerParams(
            collective_id=0, has_side_effects=True, vmem_limit_bytes=60 * 1024 * 1024
        ),
        name="parareal",
    )(state, waveform, conductivity, layer_map, loop_mask)


def solution(mesh):
    placed = (
        P("tm", None, "gx", "gy", None),
        P("tm", None),
        P(),
        P("gx", "gy", None),
        P("gx", "gy", None),
    )
    return jax.shard_map(
        body, mesh=mesh, in_specs=placed, out_specs=P("tm", None, "gx", "gy", None), check_vma=False
    )
```

```python
import jax
import jax.numpy as jnp
from jax import lax
from jax.experimental import pallas as pl
from jax.experimental.pallas import tpu as pltpu
from jax.sharding import PartitionSpec as P

DT = 0.015
GROUP = 8
MESH = pl.DeviceIdType.MESH
HIGHEST = lax.Precision.HIGHEST
DIRS = [(-1, 0), (1, 0), (-1, -1), (1, 1), (-1, 1), (1, -1), (0, -1), (0, 1)]
F32 = jnp.float32


def shifts(rows, depth):
    cell = lax.rem(lax.broadcasted_iota(jnp.int32, (rows, 128), 1), depth)
    keep_up = cell < depth - 1
    keep_down = cell > 0

    def col_next(x):
        return pltpu.roll(x, rows - 1, 0)

    def col_prev(x):
        return pltpu.roll(x, 1, 0)

    def z_next(x):
        return jnp.where(keep_up, pltpu.roll(x, 127, 1), 0.0)

    def z_prev(x):
        return jnp.where(keep_down, pltpu.roll(x, 1, 1), 0.0)

    return col_next, col_prev, z_next, z_prev


def sweep(src, dst, low, high, finish):
    col_next, col_prev, z_next, z_prev = shifts(24, 128)

    def twists(i):
        v0, v1, v2 = src[0, i], src[1, i], src[2, i]
        h1 = (z_next(v0) - v0) - (src[2, i + 1] - v2)
        h2 = (src[1, i + 1] - v1) - (col_next(v0) - v0)
        return v0, v1, v2, h1, h2

    def row(i, carry):
        h1_before, h2_before = carry
        v0, v1, v2, h1, h2 = twists(i)
        h0 = (col_next(v2) - v2) - (z_next(v1) - v1)
        k0 = (h2 - col_prev(h2)) - (h1 - z_prev(h1))
        k1 = (h0 - z_prev(h0)) - (h2 - h2_before)
        k2 = (h1 - h1_before) - (h0 - col_prev(h0))
        finish(dst, i, (v0, v1, v2), (k0, k1, k2))
        return h1, h2

    before = twists(low - 1)
    carry = (before[3], before[4])

    def rows(t, carry):
        for k in range(GROUP):
            carry = row(low + GROUP * t + k, carry)
        return carry

    groups, rest = divmod(high - low, GROUP)
    carry = lax.fori_loop(0, groups, rows, carry)
    for k in range(rest):
        carry = row(low + GROUP * groups + k, carry)


def folded_sweep(src, dst, low, width, finish):
    col_next, col_prev, z_next, z_prev = shifts(width, 64)
    left = lax.broadcasted_iota(jnp.int32, (width, 128), 1) < 64

    def load(c, p):
        return src[c, p, 0:width]

    def row_next(c, p, x):
        after = load(c, p + 1) if p < 11 else pltpu.roll(x, 64, 1)
        return jnp.where(left, after, load(c, p - 1) if p >= low else x)

    def twists(p):
        v0, v1, v2 = load(0, p), load(1, p), load(2, p)
        h1 = (z_next(v0) - v0) - (row_next(2, p, v2) - v2)
        h2 = (row_next(1, p, v1) - v1) - (col_next(v0) - v0)
        return (v0, v1, v2), h1, h2

    before, now = twists(low - 1), twists(low)
    for p in range(low, 12):
        values, h1, h2 = now
        if p < 11:
            after = twists(p + 1)
        else:
            after = (None, pltpu.roll(h1, 64, 1), pltpu.roll(h2, 64, 1))
        v0, v1, v2 = values
        h0 = (col_next(v2) - v2) - (z_next(v1) - v1)
        k0 = (h2 - col_prev(h2)) - (h1 - z_prev(h1))
        k1 = (h0 - z_prev(h0)) - (h2 - jnp.where(left, before[2], after[2]))
        k2 = (h1 - jnp.where(left, before[1], after[1])) - (h0 - col_prev(h0))
        finish(dst, p, values, (k0, k1, k2))
        before, now = now, after


def restrict(read, comps, sums):
    for half in range(2):
        for c in range(comps):
            for k in range(4):
                i = 2 * (7 - k if half else k)
                sums[half, c, k] = (read(c, i, 0) + read(c, i, 1)) + (read(c, i + 1, 0) + read(c, i + 1, 1))
    z = lax.broadcasted_iota(jnp.int32, (128, 128), 0)
    lane = lax.broadcasted_iota(jnp.int32, (128, 128), 1)
    total = 0.0
    for half in range(2):
        pick = jnp.where(lane == z // 2 + 64 * half, 0.125, 0.0).astype(F32)
        x = sums[half, 0:comps].reshape(comps * 32, 128)
        total = total + jnp.dot(x, pick, precision=HIGHEST, preferred_element_type=F32)
    return total.reshape(comps, 4, 8, 128)


def kernel(
    state, wave, cond, layer, mask, out,
    w, v, near, far, lay, msk, sums, ck, exs, exa, exb, ps, arrived, straight, zs, zarr, c0, c1, lead, ckf, ckn, acc, held,
    in_sem, fine_send, fine_recv, ck_send, ck_recv, a_send, a_recv, b_send, b_recv, s_send, s_recv, p_send, p_recv,
    z_send, z_recv, d_recv, answers, whole,
):
    n, gx, gy = lax.axis_index("tm"), lax.axis_index("gx"), lax.axis_index("gy")
    slices = 16

    plane, column = n // 4, lax.rem(n, 4)

    def beside(di, dj):
        return (n, gx + di, gy + dj)

    def exists(di, dj):
        return (gx + di >= 0) & (gx + di < 4) & (gy + dj >= 0) & (gy + dj < 4)

    def along(planes, columns):
        return (4 * lax.rem(plane + planes + 4, 4) + lax.rem(column + columns + 4, 4), gx, gy)

    def remote(src, dst, ssem, rsem, device):
        return pltpu.make_async_remote_copy(
            src_ref=src, dst_ref=dst, send_sem=ssem, recv_sem=rsem, device_id=device, device_id_type=MESH
        )

    barrier = pltpu.get_barrier_semaphore()
    for step in (1, 2, 3):

        @pl.when(column + step < 4)
        def _(step=step):
            pl.semaphore_signal(barrier, inc=1, device_id=along(0, step), device_id_type=MESH)

        @pl.when(plane + step < 4)
        def _(step=step):
            pl.semaphore_signal(barrier, inc=1, device_id=along(step, 0), device_id_type=MESH)

    for di, dj in DIRS:

        @pl.when(exists(di, dj))
        def _(di=di, dj=dj):
            pl.semaphore_signal(barrier, inc=1, device_id=beside(di, dj), device_id_type=MESH)

    loads = [
        pltpu.make_async_copy(state.at[0], w.at[0:3, 4:20, 0:16], in_sem.at[0]),
        pltpu.make_async_copy(layer, lay, in_sem.at[1]),
        pltpu.make_async_copy(mask, msk, in_sem.at[2]),
    ]
    for load in loads:
        load.start()

    @pl.when(gx == 0)
    def _():
        for buf in (ck, exs, exa, exb):
            buf[0] = jnp.zeros(buf.shape[1:], F32)

    @pl.when(gx == 3)
    def _():
        for buf in (ck, exs, exa, exb):
            buf[2] = jnp.zeros(buf.shape[1:], F32)

    @pl.when(gy == 0)
    def _():
        for buf in (ck, exs, exa, exb):
            buf[:, 0] = jnp.zeros((3,) + buf.shape[2:], F32)
        far[1] = jnp.zeros(far.shape[1:], F32)

    @pl.when(gy == 3)
    def _():
        for buf in (ck, exs, exa, exb):
            buf[:, 2] = jnp.zeros((3,) + buf.shape[2:], F32)
        far[0] = jnp.zeros(far.shape[1:], F32)

    for load in loads:
        load.wait()

    for i in range(16):
        chosen = jnp.full((16, 128), cond[0], F32)
        for level in range(1, 16):
            chosen = jnp.where(lay[i] == level, cond[level], chosen)
        scaled = DT / chosen
        w[3, 4 + i, 0:16] = scaled
        w[4, 4 + i, 0:16] = scaled * msk[i].astype(F32)
    near[0] = w[:, 4:20, 0:4]
    near[1] = w[:, 4:20, 12:16]

    two, three = jnp.int32(2), jnp.int32(3)
    in_x = jnp.where((gx == 0) | (gx == 3), two, three)
    in_y = jnp.where((gy == 0) | (gy == 3), two, three)
    pl.semaphore_wait(barrier, in_x * in_y - 1 + plane + column)

    def fine_ends(di, dj):
        if dj == 0:
            return (w.at[:, 4:8, 0:16], w.at[:, 20:24, 0:16]) if di < 0 else (w.at[:, 16:20, 0:16], w.at[:, 0:4, 0:16])
        side = 0 if dj < 0 else 1
        if di == 0:
            return near.at[side], far.at[side, :, 4:20]
        if di < 0:
            return near.at[side, :, 0:4], far.at[side, :, 20:24]
        return near.at[side, :, 12:16], far.at[side, :, 0:4]

    def swap(ends, ssem, rsem):
        copies = []
        for k, (di, dj) in enumerate(DIRS):
            source, target = ends(di, dj)
            copies.append((remote(source, target, ssem.at[k], rsem.at[k], beside(di, dj)), di, dj))

        def start():
            for copy, di, dj in copies:
                pl.when(exists(di, dj))(copy.start)

        def finish():
            for copy, di, dj in copies:
                pl.when(exists(-di, -dj))(copy.wait_recv)
            for copy, di, dj in copies:
                pl.when(exists(di, dj))(copy.wait_send)

        return start, finish

    def exchange(buf, ssem, rsem):
        return swap(lambda di, dj: (buf.at[1, 1], buf.at[1 - di, 1 - dj]), ssem, rsem)

    fine_start, fine_arrive = swap(fine_ends, fine_send, fine_recv)
    fine_start()
    for step in (1, 2, 3):

        @pl.when(column - step >= 0)
        def _(step=step):
            pl.semaphore_signal(answers.at[step - 1], inc=1, device_id=along(0, -step), device_id_type=MESH)

        @pl.when(plane - step >= 0)
        def _(step=step):
            pl.semaphore_signal(answers.at[3], inc=1, device_id=along(-step, 0), device_id_type=MESH)

    ck[1, 1] = restrict(lambda c, i, b: w[3, 4 + i, pl.ds(b, 8, stride=2)], 1, sums)[0]
    ck_start, ck_arrive = exchange(ck, ck_send, ck_recv)
    ck_start()
    exs[1, 1] = restrict(lambda c, i, b: w[c, 4 + i, pl.ds(b, 8, stride=2)], 3, sums)
    s_start, s_arrive = exchange(exs, s_send, s_recv)
    s_start()

    fine_arrive()
    for c in range(5):
        w[c, :, 16:20] = far[0, c]
        w[c, :, 20:24] = far[1, c]

    @pl.when(gx == 0)
    def _():
        w[:, 0:4] = jnp.zeros((5, 4, 24, 128), F32)

    @pl.when(gx == 3)
    def _():
        w[:, 20:24] = jnp.zeros((5, 4, 24, 128), F32)

    for step in range(4):
        pulse = wave[0, step]

        def finish(dst, i, values, curls, pulse=pulse):
            scaled = w[3, i]
            dst[0, i] = values[0] - scaled * curls[0] - pulse * w[4, i]
            dst[1, i] = values[1] - scaled * curls[1]
            dst[2, i] = values[2] - scaled * curls[2]

        src, dst = (w, v) if step % 2 == 0 else (v, w)
        sweep(src, dst, 1 + step, 23 - step, finish)

    end = restrict(lambda c, i, b: w[c, 4 + i, pl.ds(b, 8, stride=2)], 3, sums)
    exa[1, 1] = end
    a_start, a_arrive = exchange(exa, a_send, a_recv)
    a_start()
    for step in (1, 2, 3):

        @pl.when(column + step < 4)
        def _(step=step):
            pl.semaphore_wait(answers.at[step - 1], 1)

    @pl.when(plane < 3)
    def _():
        pl.semaphore_wait(answers.at[3], 3 - plane)

    for step in (1, 2, 3):
        pl.semaphore_signal(whole, inc=1, device_id=along(0, step), device_id_type=MESH)
    b_start, b_arrive = exchange(exb, b_send, b_recv)

    left_half = lax.broadcasted_iota(jnp.int32, (8, 128), 1) < 64

    def fold(read, put):
        for tile, ej in enumerate((0, 1, -1)):
            for k in range(4):
                up, down = read(-1, ej, k), read(1, ej, k)
                put(k, tile, jnp.where(left_half, up, down))
                put(7 - k, tile, pltpu.roll(jnp.where(left_half, down, up), 64, 1))
                put(8 + k, tile, read(0, ej, k))

    ck_arrive()
    def put_kappa(row, tile, block):
        ckf[row, 8 * tile : 8 * tile + 8] = block

    fold(lambda ei, ej, k: ck[ei + 1, ej + 1, k], put_kappa)

    def unpack(buf, less=None):
        for c in range(3):

            def put(row, tile, block, c=c):
                columns = slice(8 * tile, 8 * tile + 8)
                c0[c, row, columns] = block if less is None else block - less[c, row, columns]

            fold(lambda ei, ej, k, c=c: buf[ei + 1, ej + 1, c, k], put)

    def finish_coarse(dst, i, values, curls):
        scaled = ckf[i]
        for c in range(3):
            dst[c, i] = values[c] - scaled * curls[c]

    right_side = lax.broadcasted_iota(jnp.int32, (8, 128), 0) < 4

    def finish_narrow(dst, i, values, curls):
        scaled = ckn[i]
        for c in range(3):
            dst[c, i, 0:16] = values[c] - scaled * curls[c]

    def narrow(buf):
        for c in range(3):
            for p in range(4, 12):
                buf[c, p, 8:16] = jnp.where(right_side, buf[c, p, 8:16], buf[c, p, 16:24])

    for p in range(4, 12):
        ckn[p, 0:8] = ckf[p, 0:8]
        ckn[p, 8:16] = jnp.where(right_side, ckf[p, 8:16], ckf[p, 16:24])

    def carried(b):
        return jnp.where(column + b >= 4, jnp.int32(1), jnp.int32(0))

    def power(m):
        over = carried(m % 4)

        def to(buf, sem, target):
            return remote(ps.at[m - 1], buf, p_send.at[m - 1], sem, target)

        ahead = (lax.rem(n + m, slices), gx, gy)
        if m > 11:
            return [(to(arrived.at[m - 1], p_recv.at[m - 1], ahead), n + m < slices, n - m >= 0)]
        planes = m // 4 + over
        along_y = to(arrived.at[m - 1], p_recv.at[m - 1], along(planes, 0))
        if m < 9:
            return [(along_y, (planes > 0) & (plane + planes < 4), (planes > 0) & (plane - planes >= 0))]
        b = m - 8
        direct = to(straight.at[b - 1], d_recv.at[b - 1], ahead)
        return [
            (along_y, (over == 0) & (plane < 2), (over == 0) & (plane >= 2)),
            (direct, (over == 1) & (n + m < slices), (column < b) & (n - m >= 0)),
        ]

    def one(src, dst, low, m):
        @pl.when(n + m < slices)
        def _():
            if low == 5:
                narrow(src)
            if low < 5:
                folded_sweep(src, dst, low, 24, finish_coarse)
            else:
                folded_sweep(src, dst, low, 16, finish_narrow)
            ps[m - 1] = dst[:, 8:12, 0:8]
            if m != 4:
                for copy, sent, _ in power(m):
                    pl.when(sent)(copy.start)

    s_arrive()
    unpack(exs)
    folded_sweep(c0, lead, 1, 24, finish_coarse)

    @pl.when(n == 0)
    def _():
        lead[...] = jnp.zeros_like(lead)

    a_arrive()
    unpack(exa, lead)
    for m in range(1, 8):
        src, dst = (c0, c1) if m % 2 else (c1, c0)
        one(src, dst, m + 1, m)

    @pl.when(n < slices - 8)
    def _():
        exb[1, 1] = ps[6]
        b_start()

    copy, sent, _ = power(4)[0]
    pl.when(sent)(copy.start)

    def across(b):
        return remote(zs.at[b - 1], zarr.at[b - 1], z_send.at[b - 1], z_recv.at[b - 1], along(0, b))

    def relay(b):
        @pl.when(carried(b) == 0)
        def _():
            zs[b - 1] = ps[b - 1]

        @pl.when(carried(b) == 1)
        def _():
            zs[b - 1] = jnp.zeros(zs.shape[1:], F32)

        for m in (b, b + 4, b + 8):
            copy, _, received = power(m)[0]

            @pl.when(received)
            def _(copy=copy, m=m):
                copy.wait_recv()
                zs[b - 1] += arrived[m - 1]

        pl.when(plane >= carried(b))(across(b).start)

    for b in (2, 1, 3):

        @pl.when(carried(b) == 1)
        def _(b=b):
            relay(b)

    for b in (2, 1, 3):

        @pl.when(carried(b) == 0)
        def _(b=b):
            relay(b)

    pl.semaphore_wait(whole, 3)

    @pl.when(n < slices - 8)
    def _():
        b_arrive()
        unpack(exb)
        for m in range(8, slices):
            src, dst = (c1, c0) if m % 2 else (c0, c1)
            one(src, dst, m - 7, m)

    acc[...] = -lead[:, 8:12, 0:8]
    def take(copy, received, block):
        @pl.when(received)
        def _():
            copy.wait_recv()
            acc[...] += block[...]

    for m in (4, 8):
        copy, _, received = power(m)[0]
        take(copy, received, arrived.at[m - 1])
    for b in (1, 2, 3):
        take(across(b), (column >= b) | (plane > 0), zarr.at[b - 1])
    for m in (9, 10, 11):
        copy, _, received = power(m)[1]
        take(copy, received, straight.at[m - 9])
    for m in (12, 13, 14, 15):
        copy, _, received = power(m)[0]
        take(copy, received, arrived.at[m - 1])

    z = lax.broadcasted_iota(jnp.int32, (128, 128), 1)
    lane = lax.broadcasted_iota(jnp.int32, (128, 128), 0)
    packed = acc[...].reshape(96, 128)
    wide = []
    for half in range(2):
        pick = jnp.where(lane == z // 2 + 64 * half, 1.0, 0.0).astype(F32)
        wide.append(jnp.dot(packed, pick, precision=HIGHEST, preferred_element_type=F32).reshape(3, 4, 8, 128))
    stores = []
    for c in range(3):
        for half in range(2):
            for k in range(4):
                for a in range(2):
                    i = 2 * (7 - k if half else k) + a
                    for b in range(2):
                        cells = pl.ds(b, 8, stride=2)
                        held[c, i, cells] = w[c, 4 + i, cells] + wide[half][c, k]
        stores.append(pltpu.make_async_copy(held.at[c], out.at[0, c], in_sem.at[c]))
        stores[c].start()

    for m in range(1, slices):
        for copy, sent, _ in power(m):
            pl.when(sent)(copy.wait_send)
    for b in (1, 2, 3):
        pl.when(plane >= carried(b))(across(b).wait_send)
    for store in stores:
        store.wait()


def body(state, waveform, conductivity, layer_map, loop_mask):
    any_space = pl.BlockSpec(memory_space=pl.ANY)
    smem = pl.BlockSpec(memory_space=pltpu.SMEM)
    vmem = lambda *shape: pltpu.VMEM(shape, F32)
    dma = lambda count: pltpu.SemaphoreType.DMA((count,))
    return pl.pallas_call(
        kernel,
        out_shape=jax.ShapeDtypeStruct(state.shape, F32),
        in_specs=[any_space, smem, smem, any_space, any_space],
        out_specs=any_space,
        scratch_shapes=[
            vmem(5, 24, 24, 128),
            vmem(3, 24, 24, 128),
            vmem(2, 5, 16, 4, 128),
            vmem(2, 5, 24, 4, 128),
            pltpu.VMEM((16, 16, 128), jnp.int32),
            pltpu.VMEM((16, 16, 128), jnp.int32),
            vmem(2, 3, 4, 8, 128),
            vmem(3, 3, 4, 8, 128),
            vmem(3, 3, 3, 4, 8, 128),
            vmem(3, 3, 3, 4, 8, 128),
            vmem(3, 3, 3, 4, 8, 128),
            vmem(16, 3, 4, 8, 128),
            vmem(16, 3, 4, 8, 128),
            vmem(3, 3, 4, 8, 128),
            vmem(3, 3, 4, 8, 128),
            vmem(3, 3, 4, 8, 128),
            vmem(3, 12, 24, 128),
            vmem(3, 12, 24, 128),
            vmem(3, 12, 24, 128),
            vmem(12, 24, 128),
            vmem(12, 16, 128),
            vmem(3, 4, 8, 128),
            vmem(3, 16, 16, 128),
            dma(3),
            dma(8), dma(8), dma(8), dma(8), dma(8), dma(8), dma(8), dma(8),
            dma(8), dma(8), dma(16), dma(16), dma(3), dma(3), dma(3), pltpu.SemaphoreType.REGULAR((4,)), pltpu.SemaphoreType.REGULAR,
        ],
        compiler_params=pltpu.CompilerParams(
            collective_id=0, has_side_effects=True, vmem_limit_bytes=60 * 1024 * 1024
        ),
        name="parareal",
    )(state, waveform, conductivity, layer_map, loop_mask)


def solution(mesh):
    placed = (
        P("tm", None, "gx", "gy", None),
        P("tm", None),
        P(),
        P("gx", "gy", None),
        P("gx", "gy", None),
    )
    return jax.shard_map(
        body, mesh=mesh, in_specs=placed, out_specs=P("tm", None, "gx", "gy", None), check_vma=False
    )
```

```python
import jax
import jax.numpy as jnp
from jax import lax
from jax.experimental import pallas as pl
from jax.experimental.pallas import tpu as pltpu
from jax.sharding import PartitionSpec as P

DT = 0.015
GROUP = 8
MESH = pl.DeviceIdType.MESH
HIGHEST = lax.Precision.HIGHEST
DIRS = [(-1, -1), (1, 1), (-1, 1), (1, -1), (-1, 0), (1, 0), (0, -1), (0, 1)]
F32 = jnp.float32


def shifts(rows, depth):
    cell = lax.rem(lax.broadcasted_iota(jnp.int32, (rows, 128), 1), depth)
    keep_up = cell < depth - 1
    keep_down = cell > 0

    def col_next(x):
        return pltpu.roll(x, rows - 1, 0)

    def col_prev(x):
        return pltpu.roll(x, 1, 0)

    def z_next(x):
        return jnp.where(keep_up, pltpu.roll(x, 127, 1), 0.0)

    def z_prev(x):
        return jnp.where(keep_down, pltpu.roll(x, 1, 1), 0.0)

    return col_next, col_prev, z_next, z_prev


def sweep(src, dst, low, high, finish):
    col_next, col_prev, z_next, z_prev = shifts(24, 128)

    def twists(i):
        v0, v1, v2 = src[0, i], src[1, i], src[2, i]
        h1 = (z_next(v0) - v0) - (src[2, i + 1] - v2)
        h2 = (src[1, i + 1] - v1) - (col_next(v0) - v0)
        return v0, v1, v2, h1, h2

    def row(i, carry):
        h1_before, h2_before = carry
        v0, v1, v2, h1, h2 = twists(i)
        h0 = (col_next(v2) - v2) - (z_next(v1) - v1)
        k0 = (h2 - col_prev(h2)) - (h1 - z_prev(h1))
        k1 = (h0 - z_prev(h0)) - (h2 - h2_before)
        k2 = (h1 - h1_before) - (h0 - col_prev(h0))
        finish(dst, i, (v0, v1, v2), (k0, k1, k2))
        return h1, h2

    before = twists(low - 1)
    carry = (before[3], before[4])

    def rows(t, carry):
        for k in range(GROUP):
            carry = row(low + GROUP * t + k, carry)
        return carry

    groups, rest = divmod(high - low, GROUP)
    carry = lax.fori_loop(0, groups, rows, carry)
    for k in range(rest):
        carry = row(low + GROUP * groups + k, carry)


def folded_sweep(src, dst, low, width, finish):
    col_next, col_prev, z_next, z_prev = shifts(width, 64)
    left = lax.broadcasted_iota(jnp.int32, (width, 128), 1) < 64

    def load(c, p):
        return src[c, p, 0:width]

    def row_next(c, p, x):
        after = load(c, p + 1) if p < 11 else pltpu.roll(x, 64, 1)
        return jnp.where(left, after, load(c, p - 1) if p >= low else x)

    def twists(p):
        v0, v1, v2 = load(0, p), load(1, p), load(2, p)
        h1 = (z_next(v0) - v0) - (row_next(2, p, v2) - v2)
        h2 = (row_next(1, p, v1) - v1) - (col_next(v0) - v0)
        return (v0, v1, v2), h1, h2

    before, now = twists(low - 1), twists(low)
    for p in range(low, 12):
        values, h1, h2 = now
        if p < 11:
            after = twists(p + 1)
        else:
            after = (None, pltpu.roll(h1, 64, 1), pltpu.roll(h2, 64, 1))
        v0, v1, v2 = values
        h0 = (col_next(v2) - v2) - (z_next(v1) - v1)
        k0 = (h2 - col_prev(h2)) - (h1 - z_prev(h1))
        k1 = (h0 - z_prev(h0)) - (h2 - jnp.where(left, before[2], after[2]))
        k2 = (h1 - jnp.where(left, before[1], after[1])) - (h0 - col_prev(h0))
        finish(dst, p, values, (k0, k1, k2))
        before, now = now, after


def restrict(read, comps, sums):
    for half in range(2):
        for c in range(comps):
            for k in range(4):
                i = 2 * (7 - k if half else k)
                sums[half, c, k] = (read(c, i, 0) + read(c, i, 1)) + (read(c, i + 1, 0) + read(c, i + 1, 1))
    z = lax.broadcasted_iota(jnp.int32, (128, 128), 0)
    lane = lax.broadcasted_iota(jnp.int32, (128, 128), 1)
    total = 0.0
    for half in range(2):
        pick = jnp.where(lane == z // 2 + 64 * half, 0.125, 0.0).astype(F32)
        x = sums[half, 0:comps].reshape(comps * 32, 128)
        total = total + jnp.dot(x, pick, precision=HIGHEST, preferred_element_type=F32)
    return total.reshape(comps, 4, 8, 128)


def kernel(
    state, wave, cond, layer, mask, out,
    w, v, near, far, lay, msk, sums, ck, exs, exa, exb, ps, arrived, straight, zs, zarr, c0, c1, lead, ckf, ckn, acc, held,
    in_sem, fine_send, fine_recv, ck_send, ck_recv, a_send, a_recv, b_send, b_recv, s_send, s_recv, p_send, p_recv,
    z_send, z_recv, d_recv, answers, whole,
):
    n, gx, gy = lax.axis_index("tm"), lax.axis_index("gx"), lax.axis_index("gy")
    slices = 16

    plane, column = n // 4, lax.rem(n, 4)

    def beside(di, dj):
        return (n, gx + di, gy + dj)

    def exists(di, dj):
        return (gx + di >= 0) & (gx + di < 4) & (gy + dj >= 0) & (gy + dj < 4)

    def along(planes, columns):
        return (4 * lax.rem(plane + planes + 4, 4) + lax.rem(column + columns + 4, 4), gx, gy)

    def remote(src, dst, ssem, rsem, device):
        return pltpu.make_async_remote_copy(
            src_ref=src, dst_ref=dst, send_sem=ssem, recv_sem=rsem, device_id=device, device_id_type=MESH
        )

    barrier = pltpu.get_barrier_semaphore()
    for step in (1, 2, 3):

        @pl.when(column + step < 4)
        def _(step=step):
            pl.semaphore_signal(barrier, inc=1, device_id=along(0, step), device_id_type=MESH)

        @pl.when(plane + step < 4)
        def _(step=step):
            pl.semaphore_signal(barrier, inc=1, device_id=along(step, 0), device_id_type=MESH)

    for di, dj in DIRS:

        @pl.when(exists(di, dj))
        def _(di=di, dj=dj):
            pl.semaphore_signal(barrier, inc=1, device_id=beside(di, dj), device_id_type=MESH)

    loads = [
        pltpu.make_async_copy(state.at[0], w.at[0:3, 4:20, 0:16], in_sem.at[0]),
        pltpu.make_async_copy(layer, lay, in_sem.at[1]),
        pltpu.make_async_copy(mask, msk, in_sem.at[2]),
    ]
    for load in loads:
        load.start()

    @pl.when(gx == 0)
    def _():
        for buf in (ck, exs, exa, exb):
            buf[0] = jnp.zeros(buf.shape[1:], F32)

    @pl.when(gx == 3)
    def _():
        for buf in (ck, exs, exa, exb):
            buf[2] = jnp.zeros(buf.shape[1:], F32)

    @pl.when(gy == 0)
    def _():
        for buf in (ck, exs, exa, exb):
            buf[:, 0] = jnp.zeros((3,) + buf.shape[2:], F32)
        far[1] = jnp.zeros(far.shape[1:], F32)

    @pl.when(gy == 3)
    def _():
        for buf in (ck, exs, exa, exb):
            buf[:, 2] = jnp.zeros((3,) + buf.shape[2:], F32)
        far[0] = jnp.zeros(far.shape[1:], F32)

    for load in loads:
        load.wait()

    for i in range(16):
        chosen = jnp.full((16, 128), cond[0], F32)
        for level in range(1, 16):
            chosen = jnp.where(lay[i] == level, cond[level], chosen)
        scaled = DT / chosen
        w[3, 4 + i, 0:16] = scaled
        w[4, 4 + i, 0:16] = scaled * msk[i].astype(F32)
    near[0] = w[:, 4:20, 0:4]
    near[1] = w[:, 4:20, 12:16]

    two, three = jnp.int32(2), jnp.int32(3)
    in_x = jnp.where((gx == 0) | (gx == 3), two, three)
    in_y = jnp.where((gy == 0) | (gy == 3), two, three)
    pl.semaphore_wait(barrier, in_x * in_y - 1 + plane + column)

    def fine_ends(di, dj):
        if dj == 0:
            return (w.at[:, 4:8, 0:16], w.at[:, 20:24, 0:16]) if di < 0 else (w.at[:, 16:20, 0:16], w.at[:, 0:4, 0:16])
        side = 0 if dj < 0 else 1
        if di == 0:
            return near.at[side], far.at[side, :, 4:20]
        if di < 0:
            return near.at[side, :, 0:4], far.at[side, :, 20:24]
        return near.at[side, :, 12:16], far.at[side, :, 0:4]

    def swap(ends, ssem, rsem):
        copies = []
        for k, (di, dj) in enumerate(DIRS):
            source, target = ends(di, dj)
            copies.append((remote(source, target, ssem.at[k], rsem.at[k], beside(di, dj)), di, dj))

        def start():
            for copy, di, dj in copies:
                pl.when(exists(di, dj))(copy.start)

        def finish():
            for copy, di, dj in copies:
                pl.when(exists(-di, -dj))(copy.wait_recv)
            for copy, di, dj in copies:
                pl.when(exists(di, dj))(copy.wait_send)

        return start, finish

    def exchange(buf, ssem, rsem):
        return swap(lambda di, dj: (buf.at[1, 1], buf.at[1 - di, 1 - dj]), ssem, rsem)

    fine_start, fine_arrive = swap(fine_ends, fine_send, fine_recv)
    fine_start()
    for step in (1, 2, 3):

        @pl.when(column - step >= 0)
        def _(step=step):
            pl.semaphore_signal(answers.at[step - 1], inc=1, device_id=along(0, -step), device_id_type=MESH)

        @pl.when(plane - step >= 0)
        def _(step=step):
            pl.semaphore_signal(answers.at[3], inc=1, device_id=along(-step, 0), device_id_type=MESH)

    ck[1, 1] = restrict(lambda c, i, b: w[3, 4 + i, pl.ds(b, 8, stride=2)], 1, sums)[0]
    ck_start, ck_arrive = exchange(ck, ck_send, ck_recv)
    ck_start()
    exs[1, 1] = restrict(lambda c, i, b: w[c, 4 + i, pl.ds(b, 8, stride=2)], 3, sums)
    s_start, s_arrive = exchange(exs, s_send, s_recv)

    fine_arrive()
    s_start()
    for c in range(5):
        w[c, :, 16:20] = far[0, c]
        w[c, :, 20:24] = far[1, c]

    @pl.when(gx == 0)
    def _():
        w[:, 0:4] = jnp.zeros((5, 4, 24, 128), F32)

    @pl.when(gx == 3)
    def _():
        w[:, 20:24] = jnp.zeros((5, 4, 24, 128), F32)

    for step in range(4):
        pulse = wave[0, step]

        def finish(dst, i, values, curls, pulse=pulse):
            scaled = w[3, i]
            dst[0, i] = values[0] - scaled * curls[0] - pulse * w[4, i]
            dst[1, i] = values[1] - scaled * curls[1]
            dst[2, i] = values[2] - scaled * curls[2]

        src, dst = (w, v) if step % 2 == 0 else (v, w)
        sweep(src, dst, 1 + step, 23 - step, finish)

    end = restrict(lambda c, i, b: w[c, 4 + i, pl.ds(b, 8, stride=2)], 3, sums)
    exa[1, 1] = end
    a_start, a_arrive = exchange(exa, a_send, a_recv)
    a_start()
    for step in (1, 2, 3):

        @pl.when(column + step < 4)
        def _(step=step):
            pl.semaphore_wait(answers.at[step - 1], 1)

    @pl.when(plane < 3)
    def _():
        pl.semaphore_wait(answers.at[3], 3 - plane)

    for step in (1, 2, 3):
        pl.semaphore_signal(whole, inc=1, device_id=along(0, step), device_id_type=MESH)
    b_start, b_arrive = exchange(exb, b_send, b_recv)

    left_half = lax.broadcasted_iota(jnp.int32, (8, 128), 1) < 64

    def fold(read, put):
        for tile, ej in enumerate((0, 1, -1)):
            for k in range(4):
                up, down = read(-1, ej, k), read(1, ej, k)
                put(k, tile, jnp.where(left_half, up, down))
                put(7 - k, tile, pltpu.roll(jnp.where(left_half, down, up), 64, 1))
                put(8 + k, tile, read(0, ej, k))

    ck_arrive()
    def put_kappa(row, tile, block):
        ckf[row, 8 * tile : 8 * tile + 8] = block

    fold(lambda ei, ej, k: ck[ei + 1, ej + 1, k], put_kappa)

    def unpack(buf, less=None):
        for c in range(3):

            def put(row, tile, block, c=c):
                columns = slice(8 * tile, 8 * tile + 8)
                c0[c, row, columns] = block if less is None else block - less[c, row, columns]

            fold(lambda ei, ej, k, c=c: buf[ei + 1, ej + 1, c, k], put)

    def finish_coarse(dst, i, values, curls):
        scaled = ckf[i]
        for c in range(3):
            dst[c, i] = values[c] - scaled * curls[c]

    right_side = lax.broadcasted_iota(jnp.int32, (8, 128), 0) < 4

    def finish_narrow(dst, i, values, curls):
        scaled = ckn[i]
        for c in range(3):
            dst[c, i, 0:16] = values[c] - scaled * curls[c]

    def narrow(buf):
        for c in range(3):
            for p in range(4, 12):
                buf[c, p, 8:16] = jnp.where(right_side, buf[c, p, 8:16], buf[c, p, 16:24])

    for p in range(4, 12):
        ckn[p, 0:8] = ckf[p, 0:8]
        ckn[p, 8:16] = jnp.where(right_side, ckf[p, 8:16], ckf[p, 16:24])

    def carried(b):
        return jnp.where(column + b >= 4, jnp.int32(1), jnp.int32(0))

    def power(m):
        over = carried(m % 4)

        def to(buf, sem, target):
            return remote(ps.at[m - 1], buf, p_send.at[m - 1], sem, target)

        ahead = (lax.rem(n + m, slices), gx, gy)
        if m > 11:
            return [(to(arrived.at[m - 1], p_recv.at[m - 1], ahead), n + m < slices, n - m >= 0)]
        planes = m // 4 + over
        along_y = to(arrived.at[m - 1], p_recv.at[m - 1], along(planes, 0))
        if m < 9:
            return [(along_y, (planes > 0) & (plane + planes < 4), (planes > 0) & (plane - planes >= 0))]
        b = m - 8
        direct = to(straight.at[b - 1], d_recv.at[b - 1], ahead)
        return [
            (along_y, (over == 0) & (plane < 2), (over == 0) & (plane >= 2)),
            (direct, (over == 1) & (n + m < slices), (column < b) & (n - m >= 0)),
        ]

    def one(src, dst, low, m):
        @pl.when(n + m < slices)
        def _():
            if low == 5:
                narrow(src)
            if low < 5:
                folded_sweep(src, dst, low, 24, finish_coarse)
            else:
                folded_sweep(src, dst, low, 16, finish_narrow)
            ps[m - 1] = dst[:, 8:12, 0:8]
            if m != 4:
                for copy, sent, _ in power(m):
                    pl.when(sent)(copy.start)

    s_arrive()
    unpack(exs)
    folded_sweep(c0, lead, 1, 24, finish_coarse)

    @pl.when(n == 0)
    def _():
        lead[...] = jnp.zeros_like(lead)

    a_arrive()
    unpack(exa, lead)
    for m in range(1, 8):
        src, dst = (c0, c1) if m % 2 else (c1, c0)
        one(src, dst, m + 1, m)

    @pl.when(n < slices - 8)
    def _():
        exb[1, 1] = ps[6]
        b_start()

    copy, sent, _ = power(4)[0]
    pl.when(sent)(copy.start)

    def across(b):
        return remote(zs.at[b - 1], zarr.at[b - 1], z_send.at[b - 1], z_recv.at[b - 1], along(0, b))

    def relay(b):
        @pl.when(carried(b) == 0)
        def _():
            zs[b - 1] = ps[b - 1]

        @pl.when(carried(b) == 1)
        def _():
            zs[b - 1] = jnp.zeros(zs.shape[1:], F32)

        for m in (b, b + 4, b + 8):
            copy, _, received = power(m)[0]

            @pl.when(received)
            def _(copy=copy, m=m):
                copy.wait_recv()
                zs[b - 1] += arrived[m - 1]

        pl.when(plane >= carried(b))(across(b).start)

    for b in (2, 1, 3):

        @pl.when(carried(b) == 1)
        def _(b=b):
            relay(b)

    for b in (2, 1, 3):

        @pl.when(carried(b) == 0)
        def _(b=b):
            relay(b)

    pl.semaphore_wait(whole, 3)

    @pl.when(n < slices - 8)
    def _():
        b_arrive()
        unpack(exb)
        for m in range(8, slices):
            src, dst = (c1, c0) if m % 2 else (c0, c1)
            one(src, dst, m - 7, m)

    acc[...] = -lead[:, 8:12, 0:8]
    def take(copy, received, block):
        @pl.when(received)
        def _():
            copy.wait_recv()
            acc[...] += block[...]

    for m in (4, 8):
        copy, _, received = power(m)[0]
        take(copy, received, arrived.at[m - 1])
    for b in (1, 2, 3):
        take(across(b), (column >= b) | (plane > 0), zarr.at[b - 1])
    for m in (9, 10, 11):
        copy, _, received = power(m)[1]
        take(copy, received, straight.at[m - 9])
    for m in (12, 13, 14, 15):
        copy, _, received = power(m)[0]
        take(copy, received, arrived.at[m - 1])

    z = lax.broadcasted_iota(jnp.int32, (128, 128), 1)
    lane = lax.broadcasted_iota(jnp.int32, (128, 128), 0)
    packed = acc[...].reshape(96, 128)
    wide = []
    for half in range(2):
        pick = jnp.where(lane == z // 2 + 64 * half, 1.0, 0.0).astype(F32)
        wide.append(jnp.dot(packed, pick, precision=HIGHEST, preferred_element_type=F32).reshape(3, 4, 8, 128))
    stores = []
    for c in range(3):
        for half in range(2):
            for k in range(4):
                for a in range(2):
                    i = 2 * (7 - k if half else k) + a
                    for b in range(2):
                        cells = pl.ds(b, 8, stride=2)
                        held[c, i, cells] = w[c, 4 + i, cells] + wide[half][c, k]
        stores.append(pltpu.make_async_copy(held.at[c], out.at[0, c], in_sem.at[c]))
        stores[c].start()

    for m in range(1, slices):
        for copy, sent, _ in power(m):
            pl.when(sent)(copy.wait_send)
    for b in (1, 2, 3):
        pl.when(plane >= carried(b))(across(b).wait_send)
    for store in stores:
        store.wait()


def body(state, waveform, conductivity, layer_map, loop_mask):
    any_space = pl.BlockSpec(memory_space=pl.ANY)
    smem = pl.BlockSpec(memory_space=pltpu.SMEM)
    vmem = lambda *shape: pltpu.VMEM(shape, F32)
    dma = lambda count: pltpu.SemaphoreType.DMA((count,))
    return pl.pallas_call(
        kernel,
        out_shape=jax.ShapeDtypeStruct(state.shape, F32),
        in_specs=[any_space, smem, smem, any_space, any_space],
        out_specs=any_space,
        scratch_shapes=[
            vmem(5, 24, 24, 128),
            vmem(3, 24, 24, 128),
            vmem(2, 5, 16, 4, 128),
            vmem(2, 5, 24, 4, 128),
            pltpu.VMEM((16, 16, 128), jnp.int32),
            pltpu.VMEM((16, 16, 128), jnp.int32),
            vmem(2, 3, 4, 8, 128),
            vmem(3, 3, 4, 8, 128),
            vmem(3, 3, 3, 4, 8, 128),
            vmem(3, 3, 3, 4, 8, 128),
            vmem(3, 3, 3, 4, 8, 128),
            vmem(16, 3, 4, 8, 128),
            vmem(16, 3, 4, 8, 128),
            vmem(3, 3, 4, 8, 128),
            vmem(3, 3, 4, 8, 128),
            vmem(3, 3, 4, 8, 128),
            vmem(3, 12, 24, 128),
            vmem(3, 12, 24, 128),
            vmem(3, 12, 24, 128),
            vmem(12, 24, 128),
            vmem(12, 16, 128),
            vmem(3, 4, 8, 128),
            vmem(3, 16, 16, 128),
            dma(3),
            dma(8), dma(8), dma(8), dma(8), dma(8), dma(8), dma(8), dma(8),
            dma(8), dma(8), dma(16), dma(16), dma(3), dma(3), dma(3), pltpu.SemaphoreType.REGULAR((4,)), pltpu.SemaphoreType.REGULAR,
        ],
        compiler_params=pltpu.CompilerParams(
            collective_id=0, has_side_effects=True, vmem_limit_bytes=60 * 1024 * 1024
        ),
        name="parareal",
    )(state, waveform, conductivity, layer_map, loop_mask)


def solution(mesh):
    placed = (
        P("tm", None, "gx", "gy", None),
        P("tm", None),
        P(),
        P("gx", "gy", None),
        P("gx", "gy", None),
    )
    return jax.shard_map(
        body, mesh=mesh, in_specs=placed, out_specs=P("tm", None, "gx", "gy", None), check_vma=False
    )
```

```python
import jax
import jax.numpy as jnp
from jax import lax
from jax.experimental import pallas as pl
from jax.experimental.pallas import tpu as pltpu
from jax.sharding import PartitionSpec as P

DT = 0.015
GROUP = 8
MESH = pl.DeviceIdType.MESH
HIGHEST = lax.Precision.HIGHEST
DIRS = [(-1, -1), (1, 1), (-1, 1), (1, -1), (-1, 0), (1, 0), (0, -1), (0, 1)]
F32 = jnp.float32


def shifts(rows, depth):
    cell = lax.rem(lax.broadcasted_iota(jnp.int32, (rows, 128), 1), depth)
    keep_up = cell < depth - 1
    keep_down = cell > 0

    def col_next(x):
        return pltpu.roll(x, rows - 1, 0)

    def col_prev(x):
        return pltpu.roll(x, 1, 0)

    def z_next(x):
        return jnp.where(keep_up, pltpu.roll(x, 127, 1), 0.0)

    def z_prev(x):
        return jnp.where(keep_down, pltpu.roll(x, 1, 1), 0.0)

    return col_next, col_prev, z_next, z_prev


def sweep(src, dst, low, high, finish):
    col_next, col_prev, z_next, z_prev = shifts(24, 128)

    def twists(i):
        v0, v1, v2 = src[0, i], src[1, i], src[2, i]
        h1 = (z_next(v0) - v0) - (src[2, i + 1] - v2)
        h2 = (src[1, i + 1] - v1) - (col_next(v0) - v0)
        return v0, v1, v2, h1, h2

    def row(i, carry):
        h1_before, h2_before = carry
        v0, v1, v2, h1, h2 = twists(i)
        h0 = (col_next(v2) - v2) - (z_next(v1) - v1)
        k0 = (h2 - col_prev(h2)) - (h1 - z_prev(h1))
        k1 = (h0 - z_prev(h0)) - (h2 - h2_before)
        k2 = (h1 - h1_before) - (h0 - col_prev(h0))
        finish(dst, i, (v0, v1, v2), (k0, k1, k2))
        return h1, h2

    before = twists(low - 1)
    carry = (before[3], before[4])

    def rows(t, carry):
        for k in range(GROUP):
            carry = row(low + GROUP * t + k, carry)
        return carry

    groups, rest = divmod(high - low, GROUP)
    carry = lax.fori_loop(0, groups, rows, carry)
    for k in range(rest):
        carry = row(low + GROUP * groups + k, carry)


def folded_sweep(src, dst, low, width, finish):
    col_next, col_prev, z_next, z_prev = shifts(width, 64)
    left = lax.broadcasted_iota(jnp.int32, (width, 128), 1) < 64

    def load(c, p):
        return src[c, p, 0:width]

    def row_next(c, p, x):
        after = load(c, p + 1) if p < 11 else pltpu.roll(x, 64, 1)
        return jnp.where(left, after, load(c, p - 1) if p >= low else x)

    def twists(p):
        v0, v1, v2 = load(0, p), load(1, p), load(2, p)
        h1 = (z_next(v0) - v0) - (row_next(2, p, v2) - v2)
        h2 = (row_next(1, p, v1) - v1) - (col_next(v0) - v0)
        return (v0, v1, v2), h1, h2

    before, now = twists(low - 1), twists(low)
    for p in range(low, 12):
        values, h1, h2 = now
        if p < 11:
            after = twists(p + 1)
        else:
            after = (None, pltpu.roll(h1, 64, 1), pltpu.roll(h2, 64, 1))
        v0, v1, v2 = values
        h0 = (col_next(v2) - v2) - (z_next(v1) - v1)
        k0 = (h2 - col_prev(h2)) - (h1 - z_prev(h1))
        k1 = (h0 - z_prev(h0)) - (h2 - jnp.where(left, before[2], after[2]))
        k2 = (h1 - jnp.where(left, before[1], after[1])) - (h0 - col_prev(h0))
        finish(dst, p, values, (k0, k1, k2))
        before, now = now, after


def restrict(read, comps, sums):
    for half in range(2):
        for c in range(comps):
            for k in range(4):
                i = 2 * (7 - k if half else k)
                sums[half, c, k] = (read(c, i, 0) + read(c, i, 1)) + (read(c, i + 1, 0) + read(c, i + 1, 1))
    z = lax.broadcasted_iota(jnp.int32, (128, 128), 0)
    lane = lax.broadcasted_iota(jnp.int32, (128, 128), 1)
    total = 0.0
    for half in range(2):
        pick = jnp.where(lane == z // 2 + 64 * half, 0.125, 0.0).astype(F32)
        x = sums[half, 0:comps].reshape(comps * 32, 128)
        total = total + jnp.dot(x, pick, precision=HIGHEST, preferred_element_type=F32)
    return total.reshape(comps, 4, 8, 128)


def kernel(
    state, wave, cond, layer, mask, out,
    w, v, near, far, lay, msk, sums, ck, exs, exa, exb, ps, arrived, straight, zs, zarr, c0, c1, lead, ckf, ckn, acc, held,
    in_sem, fine_send, fine_recv, ck_send, ck_recv, a_send, a_recv, b_send, b_recv, s_send, s_recv, p_send, p_recv,
    z_send, z_recv, d_recv, answers, whole,
):
    n, gx, gy = lax.axis_index("tm"), lax.axis_index("gx"), lax.axis_index("gy")
    slices = 16

    plane, column = n // 4, lax.rem(n, 4)

    def beside(di, dj):
        return (n, gx + di, gy + dj)

    def exists(di, dj):
        return (gx + di >= 0) & (gx + di < 4) & (gy + dj >= 0) & (gy + dj < 4)

    def along(planes, columns):
        return (4 * lax.rem(plane + planes + 4, 4) + lax.rem(column + columns + 4, 4), gx, gy)

    def remote(src, dst, ssem, rsem, device):
        return pltpu.make_async_remote_copy(
            src_ref=src, dst_ref=dst, send_sem=ssem, recv_sem=rsem, device_id=device, device_id_type=MESH
        )

    barrier = pltpu.get_barrier_semaphore()
    for step in (1, 2, 3):

        @pl.when(column + step < 4)
        def _(step=step):
            pl.semaphore_signal(barrier, inc=1, device_id=along(0, step), device_id_type=MESH)

        @pl.when(plane + step < 4)
        def _(step=step):
            pl.semaphore_signal(barrier, inc=1, device_id=along(step, 0), device_id_type=MESH)

    for di, dj in DIRS:

        @pl.when(exists(di, dj))
        def _(di=di, dj=dj):
            pl.semaphore_signal(barrier, inc=1, device_id=beside(di, dj), device_id_type=MESH)

    loads = [
        pltpu.make_async_copy(state.at[0], w.at[0:3, 4:20, 0:16], in_sem.at[0]),
        pltpu.make_async_copy(layer, lay, in_sem.at[1]),
        pltpu.make_async_copy(mask, msk, in_sem.at[2]),
    ]
    for load in loads:
        load.start()

    @pl.when(gx == 0)
    def _():
        for buf in (ck, exs, exa, exb):
            buf[0] = jnp.zeros(buf.shape[1:], F32)

    @pl.when(gx == 3)
    def _():
        for buf in (ck, exs, exa, exb):
            buf[2] = jnp.zeros(buf.shape[1:], F32)

    @pl.when(gy == 0)
    def _():
        for buf in (ck, exs, exa, exb):
            buf[:, 0] = jnp.zeros((3,) + buf.shape[2:], F32)
        far[1] = jnp.zeros(far.shape[1:], F32)

    @pl.when(gy == 3)
    def _():
        for buf in (ck, exs, exa, exb):
            buf[:, 2] = jnp.zeros((3,) + buf.shape[2:], F32)
        far[0] = jnp.zeros(far.shape[1:], F32)

    for load in loads:
        load.wait()

    for i in range(16):
        chosen = jnp.full((16, 128), cond[0], F32)
        for level in range(1, 16):
            chosen = jnp.where(lay[i] == level, cond[level], chosen)
        scaled = DT / chosen
        w[3, 4 + i, 0:16] = scaled
        w[4, 4 + i, 0:16] = scaled * msk[i].astype(F32)
    near[0] = w[:, 4:20, 0:4]
    near[1] = w[:, 4:20, 12:16]

    two, three = jnp.int32(2), jnp.int32(3)
    in_x = jnp.where((gx == 0) | (gx == 3), two, three)
    in_y = jnp.where((gy == 0) | (gy == 3), two, three)
    pl.semaphore_wait(barrier, in_x * in_y - 1 + plane + column)

    def fine_ends(di, dj):
        if dj == 0:
            return (w.at[:, 4:8, 0:16], w.at[:, 20:24, 0:16]) if di < 0 else (w.at[:, 16:20, 0:16], w.at[:, 0:4, 0:16])
        side = 0 if dj < 0 else 1
        if di == 0:
            return near.at[side], far.at[side, :, 4:20]
        if di < 0:
            return near.at[side, :, 0:4], far.at[side, :, 20:24]
        return near.at[side, :, 12:16], far.at[side, :, 0:4]

    def swap(ends, ssem, rsem):
        copies = []
        for k, (di, dj) in enumerate(DIRS):
            source, target = ends(di, dj)
            copies.append((remote(source, target, ssem.at[k], rsem.at[k], beside(di, dj)), di, dj))

        def start():
            for copy, di, dj in copies:
                pl.when(exists(di, dj))(copy.start)

        def finish():
            for copy, di, dj in copies:
                pl.when(exists(-di, -dj))(copy.wait_recv)

        def sent():
            for copy, di, dj in copies:
                pl.when(exists(di, dj))(copy.wait_send)

        return start, finish, sent

    def exchange(buf, ssem, rsem):
        return swap(lambda di, dj: (buf.at[1, 1], buf.at[1 - di, 1 - dj]), ssem, rsem)

    fine_start, fine_arrive, fine_sent = swap(fine_ends, fine_send, fine_recv)
    fine_start()
    for step in (1, 2, 3):

        @pl.when(column - step >= 0)
        def _(step=step):
            pl.semaphore_signal(answers.at[step - 1], inc=1, device_id=along(0, -step), device_id_type=MESH)

        @pl.when(plane - step >= 0)
        def _(step=step):
            pl.semaphore_signal(answers.at[3], inc=1, device_id=along(-step, 0), device_id_type=MESH)

    ck[1, 1] = restrict(lambda c, i, b: w[3, 4 + i, pl.ds(b, 8, stride=2)], 1, sums)[0]
    ck_start, ck_arrive, ck_sent = exchange(ck, ck_send, ck_recv)
    ck_start()
    exs[1, 1] = restrict(lambda c, i, b: w[c, 4 + i, pl.ds(b, 8, stride=2)], 3, sums)
    s_start, s_arrive, s_sent = exchange(exs, s_send, s_recv)

    fine_arrive()
    s_start()
    for c in range(5):
        w[c, :, 16:20] = far[0, c]
        w[c, :, 20:24] = far[1, c]

    @pl.when(gx == 0)
    def _():
        w[:, 0:4] = jnp.zeros((5, 4, 24, 128), F32)

    @pl.when(gx == 3)
    def _():
        w[:, 20:24] = jnp.zeros((5, 4, 24, 128), F32)

    for step in range(4):
        pulse = wave[0, step]

        def finish(dst, i, values, curls, pulse=pulse):
            scaled = w[3, i]
            dst[0, i] = values[0] - scaled * curls[0] - pulse * w[4, i]
            dst[1, i] = values[1] - scaled * curls[1]
            dst[2, i] = values[2] - scaled * curls[2]

        src, dst = (w, v) if step % 2 == 0 else (v, w)
        if step == 1:
            fine_sent()
        sweep(src, dst, 1 + step, 23 - step, finish)

    end = restrict(lambda c, i, b: w[c, 4 + i, pl.ds(b, 8, stride=2)], 3, sums)
    exa[1, 1] = end
    a_start, a_arrive, a_sent = exchange(exa, a_send, a_recv)
    a_start()
    for step in (1, 2, 3):

        @pl.when(column + step < 4)
        def _(step=step):
            pl.semaphore_wait(answers.at[step - 1], 1)

    @pl.when(plane < 3)
    def _():
        pl.semaphore_wait(answers.at[3], 3 - plane)

    for step in (1, 2, 3):
        pl.semaphore_signal(whole, inc=1, device_id=along(0, step), device_id_type=MESH)
    b_start, b_arrive, b_sent = exchange(exb, b_send, b_recv)

    left_half = lax.broadcasted_iota(jnp.int32, (8, 128), 1) < 64

    def fold(read, put):
        for tile, ej in enumerate((0, 1, -1)):
            for k in range(4):
                up, down = read(-1, ej, k), read(1, ej, k)
                put(k, tile, jnp.where(left_half, up, down))
                put(7 - k, tile, pltpu.roll(jnp.where(left_half, down, up), 64, 1))
                put(8 + k, tile, read(0, ej, k))

    ck_arrive()
    def put_kappa(row, tile, block):
        ckf[row, 8 * tile : 8 * tile + 8] = block

    fold(lambda ei, ej, k: ck[ei + 1, ej + 1, k], put_kappa)

    def unpack(buf, less=None):
        for c in range(3):

            def put(row, tile, block, c=c):
                columns = slice(8 * tile, 8 * tile + 8)
                c0[c, row, columns] = block if less is None else block - less[c, row, columns]

            fold(lambda ei, ej, k, c=c: buf[ei + 1, ej + 1, c, k], put)

    def finish_coarse(dst, i, values, curls):
        scaled = ckf[i]
        for c in range(3):
            dst[c, i] = values[c] - scaled * curls[c]

    right_side = lax.broadcasted_iota(jnp.int32, (8, 128), 0) < 4

    def finish_narrow(dst, i, values, curls):
        scaled = ckn[i]
        for c in range(3):
            dst[c, i, 0:16] = values[c] - scaled * curls[c]

    def narrow(buf):
        for c in range(3):
            for p in range(4, 12):
                buf[c, p, 8:16] = jnp.where(right_side, buf[c, p, 8:16], buf[c, p, 16:24])

    for p in range(4, 12):
        ckn[p, 0:8] = ckf[p, 0:8]
        ckn[p, 8:16] = jnp.where(right_side, ckf[p, 8:16], ckf[p, 16:24])

    def carried(b):
        return jnp.where(column + b >= 4, jnp.int32(1), jnp.int32(0))

    def power(m):
        over = carried(m % 4)

        def to(buf, sem, target):
            return remote(ps.at[m - 1], buf, p_send.at[m - 1], sem, target)

        ahead = (lax.rem(n + m, slices), gx, gy)
        if m > 11:
            return [(to(arrived.at[m - 1], p_recv.at[m - 1], ahead), n + m < slices, n - m >= 0)]
        planes = m // 4 + over
        along_y = to(arrived.at[m - 1], p_recv.at[m - 1], along(planes, 0))
        if m < 9:
            return [(along_y, (planes > 0) & (plane + planes < 4), (planes > 0) & (plane - planes >= 0))]
        b = m - 8
        direct = to(straight.at[b - 1], d_recv.at[b - 1], ahead)
        return [
            (along_y, (over == 0) & (plane < 2), (over == 0) & (plane >= 2)),
            (direct, (over == 1) & (n + m < slices), (column < b) & (n - m >= 0)),
        ]

    def one(src, dst, low, m):
        @pl.when(n + m < slices)
        def _():
            if low == 5:
                narrow(src)
            if low < 5:
                folded_sweep(src, dst, low, 24, finish_coarse)
            else:
                folded_sweep(src, dst, low, 16, finish_narrow)
            ps[m - 1] = dst[:, 8:12, 0:8]
            if m != 4:
                for copy, sent, _ in power(m):
                    pl.when(sent)(copy.start)

    s_arrive()
    unpack(exs)
    folded_sweep(c0, lead, 1, 24, finish_coarse)

    @pl.when(n == 0)
    def _():
        lead[...] = jnp.zeros_like(lead)

    a_arrive()
    unpack(exa, lead)
    for m in range(1, 8):
        src, dst = (c0, c1) if m % 2 else (c1, c0)
        one(src, dst, m + 1, m)

    @pl.when(n < slices - 8)
    def _():
        exb[1, 1] = ps[6]
        b_start()

    copy, sent, _ = power(4)[0]
    pl.when(sent)(copy.start)

    def across(b):
        return remote(zs.at[b - 1], zarr.at[b - 1], z_send.at[b - 1], z_recv.at[b - 1], along(0, b))

    def relay(b):
        @pl.when(carried(b) == 0)
        def _():
            zs[b - 1] = ps[b - 1]

        @pl.when(carried(b) == 1)
        def _():
            zs[b - 1] = jnp.zeros(zs.shape[1:], F32)

        for m in (b, b + 4, b + 8):
            copy, _, received = power(m)[0]

            @pl.when(received)
            def _(copy=copy, m=m):
                copy.wait_recv()
                zs[b - 1] += arrived[m - 1]

        pl.when(plane >= carried(b))(across(b).start)

    for b in (2, 1, 3):

        @pl.when(carried(b) == 1)
        def _(b=b):
            relay(b)

    for b in (2, 1, 3):

        @pl.when(carried(b) == 0)
        def _(b=b):
            relay(b)

    pl.semaphore_wait(whole, 3)

    @pl.when(n < slices - 8)
    def _():
        b_arrive()
        unpack(exb)
        for m in range(8, slices):
            src, dst = (c1, c0) if m % 2 else (c0, c1)
            one(src, dst, m - 7, m)

    acc[...] = -lead[:, 8:12, 0:8]
    def take(copy, received, block):
        @pl.when(received)
        def _():
            copy.wait_recv()
            acc[...] += block[...]

    for m in (4, 8):
        copy, _, received = power(m)[0]
        take(copy, received, arrived.at[m - 1])
    for b in (1, 2, 3):
        take(across(b), (column >= b) | (plane > 0), zarr.at[b - 1])
    for m in (9, 10, 11):
        copy, _, received = power(m)[1]
        take(copy, received, straight.at[m - 9])
    for m in (12, 13, 14, 15):
        copy, _, received = power(m)[0]
        take(copy, received, arrived.at[m - 1])

    z = lax.broadcasted_iota(jnp.int32, (128, 128), 1)
    lane = lax.broadcasted_iota(jnp.int32, (128, 128), 0)
    packed = acc[...].reshape(96, 128)
    wide = []
    for half in range(2):
        pick = jnp.where(lane == z // 2 + 64 * half, 1.0, 0.0).astype(F32)
        wide.append(jnp.dot(packed, pick, precision=HIGHEST, preferred_element_type=F32).reshape(3, 4, 8, 128))
    stores = []
    for c in range(3):
        for half in range(2):
            for k in range(4):
                for a in range(2):
                    i = 2 * (7 - k if half else k) + a
                    for b in range(2):
                        cells = pl.ds(b, 8, stride=2)
                        held[c, i, cells] = w[c, 4 + i, cells] + wide[half][c, k]
        stores.append(pltpu.make_async_copy(held.at[c], out.at[0, c], in_sem.at[c]))
        stores[c].start()

    for m in range(1, slices):
        for copy, sent, _ in power(m):
            pl.when(sent)(copy.wait_send)
    for b in (1, 2, 3):
        pl.when(plane >= carried(b))(across(b).wait_send)
    ck_sent()
    s_sent()
    a_sent()
    pl.when(n < slices - 8)(b_sent)
    for store in stores:
        store.wait()


def body(state, waveform, conductivity, layer_map, loop_mask):
    any_space = pl.BlockSpec(memory_space=pl.ANY)
    smem = pl.BlockSpec(memory_space=pltpu.SMEM)
    vmem = lambda *shape: pltpu.VMEM(shape, F32)
    dma = lambda count: pltpu.SemaphoreType.DMA((count,))
    return pl.pallas_call(
        kernel,
        out_shape=jax.ShapeDtypeStruct(state.shape, F32),
        in_specs=[any_space, smem, smem, any_space, any_space],
        out_specs=any_space,
        scratch_shapes=[
            vmem(5, 24, 24, 128),
            vmem(3, 24, 24, 128),
            vmem(2, 5, 16, 4, 128),
            vmem(2, 5, 24, 4, 128),
            pltpu.VMEM((16, 16, 128), jnp.int32),
            pltpu.VMEM((16, 16, 128), jnp.int32),
            vmem(2, 3, 4, 8, 128),
            vmem(3, 3, 4, 8, 128),
            vmem(3, 3, 3, 4, 8, 128),
            vmem(3, 3, 3, 4, 8, 128),
            vmem(3, 3, 3, 4, 8, 128),
            vmem(16, 3, 4, 8, 128),
            vmem(16, 3, 4, 8, 128),
            vmem(3, 3, 4, 8, 128),
            vmem(3, 3, 4, 8, 128),
            vmem(3, 3, 4, 8, 128),
            vmem(3, 12, 24, 128),
            vmem(3, 12, 24, 128),
            vmem(3, 12, 24, 128),
            vmem(12, 24, 128),
            vmem(12, 16, 128),
            vmem(3, 4, 8, 128),
            vmem(3, 16, 16, 128),
            dma(3),
            dma(8), dma(8), dma(8), dma(8), dma(8), dma(8), dma(8), dma(8),
            dma(8), dma(8), dma(16), dma(16), dma(3), dma(3), dma(3), pltpu.SemaphoreType.REGULAR((4,)), pltpu.SemaphoreType.REGULAR,
        ],
        compiler_params=pltpu.CompilerParams(
            collective_id=0, has_side_effects=True, vmem_limit_bytes=60 * 1024 * 1024
        ),
        name="parareal",
    )(state, waveform, conductivity, layer_map, loop_mask)


def solution(mesh):
    placed = (
        P("tm", None, "gx", "gy", None),
        P("tm", None),
        P(),
        P("gx", "gy", None),
        P("gx", "gy", None),
    )
    return jax.shard_map(
        body, mesh=mesh, in_specs=placed, out_specs=P("tm", None, "gx", "gy", None), check_vma=False
    )
```
